128 devices in a mesh: dp: 32 (over y, x, core), mp: 4 (over z).
Axes of the slice: x: 4, y: 4, z: 4, core: 2. Of those that a mesh axis runs over, the one named last changes fastest.
Arguments:
- grads: float32 [32, 2048, 2560], P('dp', None, 'mp'), may hold values from -125 to 125
- errors: float32 [32, 2048, 2560], P('dp', None, 'mp'), may hold values from -6 to 6
- q_init: float32 [2560, 64], P('mp'), may hold values from -6 to 6
- master: float32 [2048, 2560], P('dp', 'mp'), may hold values from -4 to 4
- m_state: float32 [2048, 2560], P('dp', 'mp'), may hold values from -4 to 4
- v_state: float32 [2048, 2560], P('dp', 'mp'), may hold values from 0.01 to 1
Outputs:
- error_new: float32 [32, 2048, 2560], P('dp', None, 'mp')
- q_new: float32 [2560, 64], P('mp')
- master_new: float32 [2048, 2560], P('dp', 'mp')
- m_new: float32 [2048, 2560], P('dp', 'mp')
- v_new: float32 [2048, 2560], P('dp', 'mp')
- weights: bfloat16 [2048, 2560], P(None, 'mp')
The draws below stay inside these ranges and needn't reach their ends.
All inputs are finite; a program needn't handle non-finite values.
Results may differ from the reference program's by a relative error of at most 0.013.
Values may be sent and summed in bfloat16 or wider, within the bound.
No kernel may reach another device: no remote copies, remote signals or barrier semaphores. Data moves between devices by JAX's collectives and lax.ppermute only.
A program may use at most 64 MiB of HBM per device.

```python
import math
import jax
import jax.numpy as jnp
from jax import lax

D = 2048
HID = 2560
RANK = 64
STEP = 100
REPLICAS = 32


def draw_grads(key, part):
    key = jax.random.fold_in(key, 11)
    keys = jax.random.split(key, 4)
    row_pos = jnp.arange(D, dtype=jnp.float32) / D
    col_pos = jnp.arange(HID, dtype=jnp.float32) / HID
    trend = 3.0 ** 0.25
    shared_weight = 0.6
    own_weight = 0.8
    common = jax.random.truncated_normal(keys[2], -5.0, 5.0, (1, D, HID), jnp.float32)
    own_part = jax.random.truncated_normal(keys[3], -5.0, 5.0, (REPLICAS, D, HID), jnp.float32)
    row_scale = 10.0 ** (jax.random.uniform(keys[0], (D,), jnp.float32) - 0.5) * trend ** (2.0 * row_pos - 1.0)
    col_scale = 10.0 ** (jax.random.uniform(keys[1], (HID,), jnp.float32) - 0.5) * trend ** (2.0 * col_pos - 1.0)
    mixed = shared_weight * common + own_weight * own_part
    return (mixed * row_scale[None, :, None] * col_scale[None, None, :]).astype(jnp.float32)


def levels(stream_key, extent, cuts, low, top_value):
    def one(position, blocks):
        draws = jax.random.uniform(jax.random.fold_in(jax.random.fold_in(stream_key, 6), position), (blocks,), jnp.float32, low / len(cuts), top_value / len(cuts))
        return jnp.repeat(jnp.exp(draws), extent[position] // blocks).reshape((-1,) + (1,) * (len(extent) - position - 1))

    level = one(*cuts[0])
    for cut in cuts[1:]:
        level = level * one(*cut)
    return level


def gaussian(rng, shape, scale, bound, pieces=(), kind=jnp.bfloat16):
    result = jax.random.normal(rng, shape, jnp.float32) * scale
    if len(pieces) > 0:
        result = levels(rng, shape, pieces, -0.22, 0.18) * result
    return jnp.clip(result, min=-bound, max=bound).astype(kind)


def setup_inputs(seed: int = 0) -> dict:
    arg_keys = jax.random.split(jax.random.key(seed), 7)
    return {
        "grads": draw_grads(jax.random.fold_in(arg_keys[6], 71), 0),
        "errors": gaussian(arg_keys[1], (REPLICAS, D, HID), 0.5, 6.0, ((0, 32), (2, 4)), jnp.float32),
        "q_init": gaussian(arg_keys[2], (HID, RANK), 1.0, 6.0, ((0, 4),), jnp.float32),
        "master": gaussian(arg_keys[3], (D, HID), 0.3, 4.0, ((0, 32), (1, 4)), jnp.float32),
        "m_state": gaussian(arg_keys[4], (D, HID), 0.3, 4.0, ((0, 32), (1, 4)), jnp.float32),
        "v_state": jnp.clip(jnp.exp(math.log(1.0) - 4.6051702 * jax.random.uniform(arg_keys[5], (D, HID), jnp.float32) ** levels(arg_keys[5], (D, HID), ((0, 32), (1, 4)), -0.2, 0.2)), 0.01, 1.0),
    }


beta_first = 0.9
beta_second = 0.95
learning_rate = 0.01
decay_weight = 0.1
adam_eps = 1e-08
norm_eps = 1e-06

def orthonormalise(factor, gram_matrix):
    width = gram_matrix.shape[0]
    jitter = 1e-06 * jnp.trace(gram_matrix) / width + 1e-06
    lower_factor = jnp.linalg.cholesky(gram_matrix + jitter * jnp.eye(width, dtype=jnp.float32))
    return jax.scipy.linalg.solve_triangular(lower_factor, factor.T, lower=True).T

def reference(grads, errors, q_init, master, m_state, v_state):
    highest = lax.Precision.HIGHEST

    def left_step(running, inputs):
        gradient, buffer = inputs
        return (running + jnp.dot(gradient + buffer, q_init, precision=highest), None)
    p_sum, _ = lax.scan(left_step, jnp.zeros((D, RANK), jnp.float32), (grads, errors))
    gram_matrix = jnp.dot(p_sum.T, p_sum, precision=highest)
    p_orth = orthonormalise(p_sum, gram_matrix)

    def right_step(running, inputs):
        gradient, buffer = inputs
        return (running + jnp.dot((gradient + buffer).T, p_orth, precision=highest), None)
    q_sum, _ = lax.scan(right_step, jnp.zeros((HID, RANK), jnp.float32), (grads, errors))
    q_new = q_sum / REPLICAS
    decoded = jnp.dot(p_orth, q_new.T, precision=highest)
    error_new = grads + errors - decoded[None]
    mean_square = jnp.sum(decoded * decoded) / (D * HID)
    update = decoded / jnp.sqrt(mean_square + norm_eps)
    m_new = beta_first * m_state + (1.0 - beta_first) * update
    v_new = beta_second * v_state + (1.0 - beta_second) * update * update
    m_hat = m_new / (1.0 - beta_first ** STEP)
    v_hat = v_new / (1.0 - beta_second ** STEP)
    master_new = master * (1.0 - learning_rate * decay_weight) - learning_rate * m_hat / (jnp.sqrt(v_hat) + adam_eps)
    weights = master_new.astype(jnp.bfloat16)
    return (error_new, q_new, master_new, m_new, v_new, weights)
```

```python
import jax
import jax.numpy as jnp
from jax import lax
from jax.experimental import pallas as pl
from jax.experimental.pallas import tpu as pltpu
from jax.sharding import PartitionSpec as P

D = 2048
HID = 2560
STEP = 100
RANK = 64
REPLICAS = 32
HALF = D // 2
COLS = 640
ROWS = 64

beta_first = 0.9
beta_second = 0.95
learning_rate = 0.01
decay_weight = 0.1
adam_eps = 1e-08
norm_eps = 1e-06

f32 = jnp.float32
bf16 = jnp.bfloat16
HIGHEST = lax.Precision.HIGHEST
VMEM_BYTES = 48 * 1024 * 1024
LEFT_CHUNKS = 8
BLOCK = 256


def split(x):
    high = x.astype(bf16)
    return high, (x - high.astype(f32)).astype(bf16)


def dot(a, b, ca, cb, precision=None):
    return lax.dot_general(
        a, b, (((ca,), (cb,)), ((), ())), precision=precision, preferred_element_type=f32
    )


def lanes(shape):
    return lax.broadcasted_iota(jnp.int32, shape, len(shape) - 1)


def left_kernel(grads, errors, q_ref, merged_ref, part_ref, buffer, sems):
    size = HALF // LEFT_CHUNKS
    copies = []
    for c in range(LEFT_CHUNKS):
        rows = pl.ds(c * size, size)
        pair = (
            pltpu.make_async_copy(grads.at[:, rows], merged_ref.at[:, rows], sems.at[0, c]),
            pltpu.make_async_copy(errors.at[:, rows], buffer.at[:, rows], sems.at[1, c]),
        )
        for copy in pair:
            copy.start()
        copies.append(pair)
    q = q_ref[...]
    q_high = q.astype(bf16).astype(f32)
    right = jnp.concatenate([q_high, q - q_high], axis=1).astype(bf16)
    low_lanes = lanes((size, 2 * RANK)) < RANK
    for c in range(LEFT_CHUNKS):
        for copy in copies[c]:
            copy.wait()
        rows = pl.ds(c * size, size)
        merged = merged_ref[:, rows] + buffer[:, rows]
        merged_ref[:, rows] = merged
        high, low = split(merged.reshape(2 * size, COLS))
        part = dot(high, right, 1, 0) + dot(low, right, 1, 0)
        part = part + pltpu.roll(part, RANK, 1)
        part_ref[rows, :] = jnp.where(low_lanes, part[:size], part[size:]).astype(bf16)


def left(grads, errors, q_init):
    return pl.pallas_call(
        left_kernel,
        out_shape=(
            jax.ShapeDtypeStruct((2, HALF, COLS), f32),
            jax.ShapeDtypeStruct((HALF, 2 * RANK), bf16),
        ),
        in_specs=[
            pl.BlockSpec(memory_space=pl.ANY),
            pl.BlockSpec(memory_space=pl.ANY),
            pl.BlockSpec(memory_space=pltpu.VMEM),
        ],
        out_specs=(
            pl.BlockSpec(memory_space=pltpu.VMEM),
            pl.BlockSpec(memory_space=pltpu.VMEM),
        ),
        scratch_shapes=[
            pltpu.VMEM((2, HALF, COLS), f32),
            pltpu.SemaphoreType.DMA((2, LEFT_CHUNKS)),
        ],
        compiler_params=pltpu.CompilerParams(vmem_limit_bytes=VMEM_BYTES),
        name="left_factor",
    )(grads.reshape(2, HALF, COLS), errors.reshape(2, HALF, COLS), q_init)


def sum_kernel(parts_ref, out_ref):
    total = jnp.sum(parts_ref[...].astype(f32).reshape(out_ref.shape), axis=0, keepdims=True)
    out_ref[...] = jnp.broadcast_to(total, out_ref.shape)


def sum_repeat(parts):
    return pl.pallas_call(
        sum_kernel,
        out_shape=jax.ShapeDtypeStruct((128, 8, 128), f32),
        in_specs=[pl.BlockSpec(memory_space=pltpu.VMEM)],
        out_specs=pl.BlockSpec(memory_space=pltpu.VMEM),
        compiler_params=pltpu.CompilerParams(vmem_limit_bytes=VMEM_BYTES),
        name="sum_repeat",
    )(parts)


def inverse_factor(gram):
    row_id = lax.broadcasted_iota(jnp.int32, (RANK, 2 * RANK), 0)
    lane = lanes((RANK, 2 * RANK))
    eye = jnp.where(row_id == lane, 1.0, 0.0).astype(f32)
    trace = jnp.sum(gram * eye, keepdims=True)
    jitter = 1e-06 * trace / RANK + 1e-06
    start = jnp.where(lane < RANK, gram + jitter * eye, jnp.where(row_id == lane - RANK, 1.0, 0.0))
    tiles = [start[8 * k : 8 * k + 8] for k in range(RANK // 8)]
    sub = lax.broadcasted_iota(jnp.int32, (8, 1), 0)
    for j in range(RANK - 1):
        t, r = divmod(j, 8)
        row = tiles[t][r : r + 1]
        row = row * (1.0 / row[:, j : j + 1])
        for k in range(t, RANK // 8):
            factor = tiles[k][:, j : j + 1]
            if k == t:
                factor = jnp.where(sub > r, factor, 0.0)
            tiles[k] = tiles[k] - factor * row
    done = jnp.concatenate(tiles, axis=0)
    pivots = jnp.sum(done * eye, axis=1, keepdims=True)
    return jnp.where(lane < RANK, 0.0, done * (1.0 / jnp.sqrt(pivots)))


def pair_rows(packed):
    low_lanes = lanes(packed.shape) < RANK
    high = packed.astype(bf16).astype(f32)
    low = packed - high
    top = jnp.where(low_lanes, high, pltpu.roll(low, RANK, 1)).astype(bf16)
    bottom = jnp.where(low_lanes, pltpu.roll(high, RANK, 1), low).astype(bf16)
    return top, bottom


def right_kernel(p_ref, merged_ref, orth_ref, square_ref, part_ref):
    packed = p_ref[...]
    gram = dot(packed, packed, 0, 0, HIGHEST)
    shifted = pltpu.roll(gram[RANK:], RANK, 1)
    gram = gram[:RANK] + shifted
    inverse = inverse_factor(gram)

    pairs = pair_rows(packed)
    acc = jnp.zeros((2 * RANK, COLS), f32)
    for half in range(2):
        for c in range(4):
            rows = slice(c * BLOCK, (c + 1) * BLOCK)
            high, low = split(merged_ref[half, rows])
            acc = acc + (dot(pairs[half][rows], high, 0, 0) + dot(pairs[half][rows], low, 0, 0))
    part = acc[:RANK] + acc[RANK:]

    both = jnp.concatenate([pltpu.roll(inverse, RANK, 1), inverse], axis=0)
    inverse_small = both[:RANK, :RANK]
    part_ref[...] = (dot(inverse_small, part, 1, 0, HIGHEST) * (1.0 / REPLICAS)).astype(bf16)
    orth = dot(packed, both, 1, 1, HIGHEST)
    square = dot(orth, orth, 0, 0, HIGHEST)
    square_ref[...] = square[:RANK] + pltpu.roll(square[RANK:], RANK, 1)
    top, bottom = pair_rows(orth)
    orth_ref[:HALF] = top
    orth_ref[HALF:] = bottom


def right(packed, merged):
    return pl.pallas_call(
        right_kernel,
        out_shape=(
            jax.ShapeDtypeStruct((D, 2 * RANK), bf16),
            jax.ShapeDtypeStruct((RANK, 2 * RANK), f32),
            jax.ShapeDtypeStruct((RANK, COLS), bf16),
        ),
        in_specs=[pl.BlockSpec(memory_space=pltpu.VMEM)] * 2,
        out_specs=(pl.BlockSpec(memory_space=pltpu.VMEM),) * 3,
        compiler_params=pltpu.CompilerParams(vmem_limit_bytes=VMEM_BYTES),
        name="right_factor",
    )(packed, merged)


def adam(update, master, m_state, v_state):
    m_new = beta_first * m_state + (1.0 - beta_first) * update
    v_new = beta_second * v_state + (1.0 - beta_second) * update * update
    m_hat = m_new / (1.0 - beta_first**STEP)
    v_hat = v_new / (1.0 - beta_second**STEP)
    master_new = master * (1.0 - learning_rate * decay_weight) - learning_rate * m_hat / (
        jnp.sqrt(v_hat) + adam_eps
    )
    return m_new, v_new, master_new


def final_kernel(
    q_ref,
    orth_ref,
    square_ref,
    merged_ref,
    states_ref,
    master_ref,
    m_ref,
    v_ref,
    error_ref,
    weights_ref,
    q_out,
    master_out,
    m_out,
    v_out,
    both_ref,
    scale_ref,
):
    step = pl.program_id(0)

    @pl.when(step == 0)
    def _():
        gram = jnp.zeros((RANK, RANK), f32)
        for z in range(4):
            gram = gram + dot(q_ref[z], q_ref[z], 1, 1)
        total = jnp.sum(gram * square_ref[:, :RANK], keepdims=True)
        scale = 1.0 / jnp.sqrt(total / (D * HID) + norm_eps)
        scale_ref[...] = jnp.broadcast_to(scale, scale_ref.shape)
        q = q_ref[lax.axis_index("mp")]
        both_ref[:RANK] = q
        both_ref[RANK:] = q
        q_out[...] = q.astype(f32).T
        start = pl.multiple_of(lax.axis_index("dp") * ROWS, ROWS)
        decoded = dot(orth_ref[pl.ds(start, ROWS)], both_ref[...], 1, 0)
        m_new, v_new, master_new = adam(decoded * scale, master_ref[...], m_ref[...], v_ref[...])
        m_out[...] = m_new
        v_out[...] = v_new
        master_out[...] = master_new

    rows = pl.ds(pl.multiple_of(step * BLOCK, BLOCK), BLOCK)
    decoded = dot(orth_ref[rows], both_ref[...], 1, 0)
    error_ref[...] = merged_ref[...] - decoded
    update = decoded * scale_ref[:1, :1]
    for k in range(BLOCK // ROWS):
        part = slice(k * ROWS, (k + 1) * ROWS)
        state = [states_ref[k, n].astype(f32) for n in range(3)]
        weights_ref[part] = adam(update[part], *state)[2].astype(bf16)


def final(q_all, orth, square, merged, states, master, m_state, v_state):
    steps = D // BLOCK
    whole = lambda *shape: pl.BlockSpec(shape, lambda i: (0,) * len(shape))
    return pl.pallas_call(
        final_kernel,
        grid=(steps,),
        out_shape=(
            jax.ShapeDtypeStruct((D, COLS), f32),
            jax.ShapeDtypeStruct((D, COLS), bf16),
            jax.ShapeDtypeStruct((COLS, RANK), f32),
            jax.ShapeDtypeStruct((ROWS, COLS), f32),
            jax.ShapeDtypeStruct((ROWS, COLS), f32),
            jax.ShapeDtypeStruct((ROWS, COLS), f32),
        ),
        in_specs=[
            whole(4, RANK, COLS),
            whole(D, 2 * RANK),
            whole(RANK, 2 * RANK),
            pl.BlockSpec((BLOCK, COLS), lambda i: (i, 0)),
            pl.BlockSpec((BLOCK // ROWS, 3, ROWS, COLS), lambda i: (i, 0, 0, 0)),
            whole(ROWS, COLS),
            whole(ROWS, COLS),
            whole(ROWS, COLS),
        ],
        out_specs=(
            pl.BlockSpec((BLOCK, COLS), lambda i: (i, 0)),
            pl.BlockSpec((BLOCK, COLS), lambda i: (i, 0)),
            whole(COLS, RANK),
            whole(ROWS, COLS),
            whole(ROWS, COLS),
            whole(ROWS, COLS),
        ),
        scratch_shapes=[pltpu.VMEM((2 * RANK, COLS), bf16), pltpu.VMEM((8, 128), f32)],
        compiler_params=pltpu.CompilerParams(vmem_limit_bytes=VMEM_BYTES),
        name="decode_update",
    )(q_all, orth, square, merged, states, master, m_state, v_state)


def shards(grads, errors, q_init, master, m_state, v_state):
    states = jnp.stack([master, m_state, v_state]).astype(bf16)
    states = lax.all_gather(states, "dp", axis=0, tiled=False)
    merged, part = left(grads, errors, q_init)
    parts = lax.all_to_all(part.reshape(128, 8, 128), ("dp", "mp"), 0, 0)
    owned = sum_repeat(parts.reshape(HALF, 128))
    packed = lax.all_to_all(owned, ("dp", "mp"), 0, 0).reshape(HALF, 128)
    orth, square, q_part = right(packed, merged)
    q_parts = lax.all_to_all(q_part.reshape(32, 2, COLS), "dp", 0, 0)
    q_owned = jnp.sum(q_parts.astype(f32), axis=0).astype(bf16)
    q_owned = jnp.broadcast_to(q_owned[None], (128, 2, COLS))
    q_all = lax.all_to_all(q_owned, ("mp", "dp"), 0, 0).reshape(4, RANK, COLS)
    error_new, weights, q_new, master_new, m_new, v_new = final(
        q_all, orth, square, merged.reshape(D, COLS), states, master, m_state, v_state
    )
    return (error_new[None], q_new, master_new, m_new, v_new, weights)


def solution(mesh):
    in_specs = (
        P("dp", None, "mp"),
        P("dp", None, "mp"),
        P("mp", None),
        P("dp", "mp"),
        P("dp", "mp"),
        P("dp", "mp"),
    )
    out_specs = (
        P("dp", None, "mp"),
        P("mp", None),
        P("dp", "mp"),
        P("dp", "mp"),
        P("dp", "mp"),
        P(None, "mp"),
    )
    return jax.shard_map(shards, mesh=mesh, in_specs=in_specs, out_specs=out_specs, check_vma=False)
```

```python
import jax
import jax.numpy as jnp
from jax import lax
from jax.experimental import pallas as pl
from jax.experimental.pallas import tpu as pltpu
from jax.sharding import PartitionSpec as P

D = 2048
HID = 2560
STEP = 100
RANK = 64
REPLICAS = 32
HALF = D // 2
COLS = 640
ROWS = 64

beta_first = 0.9
beta_second = 0.95
learning_rate = 0.01
decay_weight = 0.1
adam_eps = 1e-08
norm_eps = 1e-06

f32 = jnp.float32
bf16 = jnp.bfloat16
HIGHEST = lax.Precision.HIGHEST
MIB = 1024 * 1024
LEFT_CHUNKS = 8
BLOCK = 256


def split(x):
    high = x.astype(bf16)
    return high, (x - high.astype(f32)).astype(bf16)


def dot(a, b, ca, cb, precision=None):
    return lax.dot_general(
        a, b, (((ca,), (cb,)), ((), ())), precision=precision, preferred_element_type=f32
    )


def hbm(x):
    return pltpu.with_memory_space_constraint(x, pltpu.HBM)


def lanes(shape):
    return lax.broadcasted_iota(jnp.int32, shape, len(shape) - 1)


def left_kernel(
    grads, errors, q_hbm, master, m_state, v_state,
    merged_ref, part_ref, states_ref,
    buffer, q_buffer, state_buffer, sems, small_sems,
):
    size = HALF // LEFT_CHUNKS
    small = [pltpu.make_async_copy(q_hbm, q_buffer, small_sems.at[0])]
    for n, source in enumerate((master, m_state, v_state)):
        small.append(pltpu.make_async_copy(source, state_buffer.at[n], small_sems.at[n + 1]))
    for copy in small:
        copy.start()
    copies = []
    for c in range(LEFT_CHUNKS):
        rows = pl.ds(c * size, size)
        pair = (
            pltpu.make_async_copy(grads.at[:, rows], merged_ref.at[:, rows], sems.at[0, c]),
            pltpu.make_async_copy(errors.at[:, rows], buffer.at[:, rows], sems.at[1, c]),
        )
        for copy in pair:
            copy.start()
        copies.append(pair)
    small[0].wait()
    q = q_buffer[...]
    q_high = q.astype(bf16).astype(f32)
    right = jnp.concatenate([q_high, q - q_high], axis=0).T.astype(bf16)
    for n in range(3):
        small[n + 1].wait()
        states_ref[n] = state_buffer[n].astype(bf16)
    low_lanes = lanes((size, 2 * RANK)) < RANK
    for c in range(LEFT_CHUNKS):
        for copy in copies[c]:
            copy.wait()
        rows = pl.ds(c * size, size)
        merged = merged_ref[:, rows] + buffer[:, rows]
        merged_ref[:, rows] = merged
        high, low = split(merged.reshape(2 * size, COLS))
        part = dot(high, right, 1, 0) + dot(low, right, 1, 0)
        part = part + pltpu.roll(part, RANK, 1)
        part_ref[rows, :] = jnp.where(low_lanes, part[:size], part[size:]).astype(bf16)


def left(grads, errors, q_init, master, m_state, v_state):
    return pl.pallas_call(
        left_kernel,
        out_shape=(
            jax.ShapeDtypeStruct((2, HALF, COLS), f32),
            jax.ShapeDtypeStruct((HALF, 2 * RANK), bf16),
            jax.ShapeDtypeStruct((3, ROWS, COLS), bf16),
        ),
        in_specs=[pl.BlockSpec(memory_space=pltpu.HBM)] * 6,
        out_specs=(pl.BlockSpec(memory_space=pltpu.VMEM),) * 3,
        scratch_shapes=[
            pltpu.VMEM((2, HALF, COLS), f32),
            pltpu.VMEM((RANK, COLS), f32),
            pltpu.VMEM((3, ROWS, COLS), f32),
            pltpu.SemaphoreType.DMA((2, LEFT_CHUNKS)),
            pltpu.SemaphoreType.DMA((4,)),
        ],
        compiler_params=pltpu.CompilerParams(vmem_limit_bytes=20 * MIB),
        name="left_factor",
    )(
        hbm(grads.reshape(2, HALF, COLS)), hbm(errors.reshape(2, HALF, COLS)), hbm(q_init.T),
        hbm(master), hbm(m_state), hbm(v_state),
    )


def sum_kernel(parts_ref, out_ref):
    total = jnp.sum(parts_ref[...].astype(f32).reshape(out_ref.shape), axis=0, keepdims=True)
    out_ref[...] = jnp.broadcast_to(total, out_ref.shape)


def sum_repeat(parts):
    return pl.pallas_call(
        sum_kernel,
        out_shape=jax.ShapeDtypeStruct((128, 8, 128), f32),
        in_specs=[pl.BlockSpec(memory_space=pltpu.VMEM)],
        out_specs=pl.BlockSpec(memory_space=pltpu.VMEM),
        compiler_params=pltpu.CompilerParams(vmem_limit_bytes=16 * MIB),
        name="sum_repeat",
    )(parts)


def inverse_factor(gram):
    row_id = lax.broadcasted_iota(jnp.int32, (RANK, 2 * RANK), 0)
    lane = lanes((RANK, 2 * RANK))
    eye = jnp.where(row_id == lane, 1.0, 0.0).astype(f32)
    trace = jnp.sum(gram * eye, keepdims=True)
    jitter = 1e-06 * trace / RANK + 1e-06
    start = jnp.where(lane < RANK, gram + jitter * eye, jnp.where(row_id == lane - RANK, 1.0, 0.0))
    tiles = [start[8 * k : 8 * k + 8] for k in range(RANK // 8)]
    sub = lax.broadcasted_iota(jnp.int32, (8, 1), 0)
    for j in range(RANK - 1):
        t, r = divmod(j, 8)
        row = tiles[t][r : r + 1]
        row = row * (1.0 / row[:, j : j + 1])
        for k in range(t, RANK // 8):
            factor = tiles[k][:, j : j + 1]
            if k == t:
                factor = jnp.where(sub > r, factor, 0.0)
            tiles[k] = tiles[k] - factor * row
    done = jnp.concatenate(tiles, axis=0)
    pivots = jnp.sum(done * eye, axis=1, keepdims=True)
    return jnp.where(lane < RANK, 0.0, done * (1.0 / jnp.sqrt(pivots)))


def pair_rows(packed):
    low_lanes = lanes(packed.shape) < RANK
    high = packed.astype(bf16).astype(f32)
    low = packed - high
    top = jnp.where(low_lanes, high, pltpu.roll(low, RANK, 1)).astype(bf16)
    bottom = jnp.where(low_lanes, pltpu.roll(high, RANK, 1), low).astype(bf16)
    return top, bottom


def right_kernel(p_ref, merged_ref, orth_ref, square_ref, part_ref):
    packed = p_ref[...]
    gram = dot(packed, packed, 0, 0, HIGHEST)
    shifted = pltpu.roll(gram[RANK:], RANK, 1)
    gram = gram[:RANK] + shifted
    inverse = inverse_factor(gram)

    pairs = pair_rows(packed)
    acc = jnp.zeros((2 * RANK, COLS), f32)
    for half in range(2):
        for c in range(4):
            rows = slice(c * BLOCK, (c + 1) * BLOCK)
            high, low = split(merged_ref[half, rows])
            acc = acc + (dot(pairs[half][rows], high, 0, 0) + dot(pairs[half][rows], low, 0, 0))
    part = acc[:RANK] + acc[RANK:]

    both = jnp.concatenate([pltpu.roll(inverse, RANK, 1), inverse], axis=0)
    inverse_small = both[:RANK, :RANK]
    part_ref[...] = (dot(inverse_small, part, 1, 0, HIGHEST) * (1.0 / REPLICAS)).astype(bf16)
    orth = dot(packed, both, 1, 1, HIGHEST)
    square = dot(orth, orth, 0, 0, HIGHEST)
    square_ref[...] = square[:RANK] + pltpu.roll(square[RANK:], RANK, 1)
    top, bottom = pair_rows(orth)
    orth_ref[:HALF] = top
    orth_ref[HALF:] = bottom


def right(packed, merged):
    return pl.pallas_call(
        right_kernel,
        out_shape=(
            jax.ShapeDtypeStruct((D, 2 * RANK), bf16),
            jax.ShapeDtypeStruct((RANK, 2 * RANK), f32),
            jax.ShapeDtypeStruct((RANK, COLS), bf16),
        ),
        in_specs=[pl.BlockSpec(memory_space=pltpu.VMEM)] * 2,
        out_specs=(pl.BlockSpec(memory_space=pltpu.VMEM),) * 3,
        compiler_params=pltpu.CompilerParams(vmem_limit_bytes=16 * MIB),
        name="right_factor",
    )(packed, merged)


def adam(update, master, m_state, v_state):
    m_new = beta_first * m_state + (1.0 - beta_first) * update
    v_new = beta_second * v_state + (1.0 - beta_second) * update * update
    m_hat = m_new / (1.0 - beta_first**STEP)
    v_hat = v_new / (1.0 - beta_second**STEP)
    master_new = master * (1.0 - learning_rate * decay_weight) - learning_rate * m_hat / (
        jnp.sqrt(v_hat) + adam_eps
    )
    return m_new, v_new, master_new


def new_weights(update, master, m_state, v_state):
    first = learning_rate / (1.0 - beta_first**STEP)
    second = 1.0 / (1.0 - beta_second**STEP)
    top = (first * beta_first) * m_state + (first * (1.0 - beta_first)) * update
    square = (second * beta_second) * v_state + (second * (1.0 - beta_second)) * (update * update)
    root = square * lax.rsqrt(square) + adam_eps
    return (1.0 - learning_rate * decay_weight) * master - top * pl.reciprocal(root, approx=True)


def final_kernel(
    q_ref, orth_ref, square_ref, merged_ref, states_hbm, master_ref, m_ref, v_ref,
    error_hbm, weights_hbm, q_hbm, master_hbm, m_hbm, v_hbm,
    states_ref, error_ref, weights_ref, q_out, owned_ref, both_ref,
    in_sems, error_sems, weight_sems, small_sems,
):
    steps = D // BLOCK
    per = BLOCK // ROWS

    def states_copy(c):
        part = pl.ds(c * per, per)
        return pltpu.make_async_copy(states_hbm.at[part], states_ref.at[part], in_sems.at[c])

    def out_copies(c):
        rows = pl.ds(pl.multiple_of(c * BLOCK, BLOCK), BLOCK)
        return (
            pltpu.make_async_copy(error_ref.at[rows], error_hbm.at[rows], error_sems.at[c]),
            pltpu.make_async_copy(weights_ref.at[rows], weights_hbm.at[rows], weight_sems.at[c]),
        )

    for c in range(steps):
        states_copy(c).start()
    gram = jnp.zeros((RANK, RANK), f32)
    for z in range(4):
        gram = gram + dot(q_ref[z], q_ref[z], 1, 1)
    total = jnp.sum(gram * square_ref[:, :RANK], keepdims=True)
    scale = 1.0 / jnp.sqrt(total / (D * HID) + norm_eps)
    q = q_ref[lax.axis_index("mp")]
    both_ref[:RANK] = q
    both_ref[RANK:] = q
    q_out[...] = q.astype(f32)
    start = pl.multiple_of(lax.axis_index("dp") * ROWS, ROWS)
    decoded = dot(orth_ref[pl.ds(start, ROWS)], both_ref[...], 1, 0)
    owned = adam(decoded * scale, master_ref[...], m_ref[...], v_ref[...])
    small = [pltpu.make_async_copy(q_out, q_hbm, small_sems.at[3])]
    for n, target in enumerate((m_hbm, v_hbm, master_hbm)):
        owned_ref[n] = owned[n]
        small.append(pltpu.make_async_copy(owned_ref.at[n], target, small_sems.at[n]))
    for copy in small:
        copy.start()

    @pl.loop(0, steps)
    def _(c):
        rows = pl.ds(pl.multiple_of(c * BLOCK, BLOCK), BLOCK)
        decoded = dot(orth_ref[rows], both_ref[...], 1, 0)
        error_ref[rows] = merged_ref[rows] - decoded
        update = decoded * scale
        states_copy(c).wait()
        for k in range(per):
            state = [states_ref[c * per + k, n].astype(f32) for n in range(3)]
            block = pl.ds(pl.multiple_of(c * BLOCK + k * ROWS, ROWS), ROWS)
            weights_ref[block] = new_weights(update[k * ROWS : (k + 1) * ROWS], *state).astype(bf16)
        for copy in out_copies(c):
            copy.start()

    for c in range(steps):
        for copy in out_copies(c):
            copy.wait()
    for copy in small:
        copy.wait()


def final(q_all, orth, square, merged, states, master, m_state, v_state):
    steps = D // BLOCK
    return pl.pallas_call(
        final_kernel,
        out_shape=(
            jax.ShapeDtypeStruct((D, COLS), f32),
            jax.ShapeDtypeStruct((D, COLS), bf16),
            jax.ShapeDtypeStruct((RANK, COLS), f32),
            jax.ShapeDtypeStruct((ROWS, COLS), f32),
            jax.ShapeDtypeStruct((ROWS, COLS), f32),
            jax.ShapeDtypeStruct((ROWS, COLS), f32),
        ),
        in_specs=[pl.BlockSpec(memory_space=pltpu.VMEM)] * 4
        + [pl.BlockSpec(memory_space=pltpu.HBM)]
        + [pl.BlockSpec(memory_space=pltpu.VMEM)] * 3,
        out_specs=(pl.BlockSpec(memory_space=pl.ANY),) * 6,
        scratch_shapes=[
            pltpu.VMEM((REPLICAS, 3, ROWS, COLS), bf16),
            pltpu.VMEM((D, COLS), f32),
            pltpu.VMEM((D, COLS), bf16),
            pltpu.VMEM((RANK, COLS), f32),
            pltpu.VMEM((3, ROWS, COLS), f32),
            pltpu.VMEM((2 * RANK, COLS), bf16),
            pltpu.SemaphoreType.DMA((steps,)),
            pltpu.SemaphoreType.DMA((steps,)),
            pltpu.SemaphoreType.DMA((steps,)),
            pltpu.SemaphoreType.DMA((4,)),
        ],
        compiler_params=pltpu.CompilerParams(vmem_limit_bytes=32 * MIB),
        name="decode_update",
    )(q_all, orth, square, merged, hbm(states), master, m_state, v_state)


def shards(grads, errors, q_init, master, m_state, v_state):
    merged, part, states = left(grads, errors, q_init, master, m_state, v_state)
    states = lax.all_gather(states, "dp", axis=0, tiled=False)
    parts = lax.all_to_all(part.reshape(128, 8, 128), ("dp", "mp"), 0, 0)
    owned = sum_repeat(parts.reshape(HALF, 128))
    packed = lax.all_to_all(owned, ("dp", "mp"), 0, 0).reshape(HALF, 128)
    orth, square, q_part = right(packed, merged)
    q_parts = lax.all_to_all(q_part.reshape(32, 2, COLS), "dp", 0, 0)
    q_owned = jnp.sum(q_parts.astype(f32), axis=0).astype(bf16)
    q_owned = jnp.broadcast_to(q_owned[None], (128, 2, COLS))
    q_all = lax.all_to_all(q_owned, ("mp", "dp"), 0, 0).reshape(4, RANK, COLS)
    error_new, weights, q_new, master_new, m_new, v_new = final(
        q_all, orth, square, merged.reshape(D, COLS), states, master, m_state, v_state
    )
    return (error_new[None], q_new.T, master_new, m_new, v_new, weights)


def solution(mesh):
    in_specs = (
        P("dp", None, "mp"),
        P("dp", None, "mp"),
        P("mp", None),
        P("dp", "mp"),
        P("dp", "mp"),
        P("dp", "mp"),
    )
    out_specs = (
        P("dp", None, "mp"),
        P("mp", None),
        P("dp", "mp"),
        P("dp", "mp"),
        P("dp", "mp"),
        P(None, "mp"),
    )
    return jax.shard_map(shards, mesh=mesh, in_specs=in_specs, out_specs=out_specs, check_vma=False)
```

```python
import jax
import jax.numpy as jnp
from jax import lax
from jax.experimental import pallas as pl
from jax.experimental.pallas import tpu as pltpu
from jax.sharding import PartitionSpec as P

D = 2048
HID = 2560
STEP = 100
RANK = 64
REPLICAS = 32
HALF = D // 2
COLS = 640
ROWS = 64

beta_first = 0.9
beta_second = 0.95
learning_rate = 0.01
decay_weight = 0.1
adam_eps = 1e-08
norm_eps = 1e-06

f32 = jnp.float32
bf16 = jnp.bfloat16
HIGHEST = lax.Precision.HIGHEST
MIB = 1024 * 1024
LEFT_CHUNKS = 8
AHEAD = 3
BLOCK = 256


def split(x):
    high = x.astype(bf16)
    return high, (x - high.astype(f32)).astype(bf16)


def dot(a, b, ca, cb, precision=None):
    return lax.dot_general(
        a, b, (((ca,), (cb,)), ((), ())), precision=precision, preferred_element_type=f32
    )


def hbm(x):
    return pltpu.with_memory_space_constraint(x, pltpu.HBM)


def lanes(shape):
    return lax.broadcasted_iota(jnp.int32, shape, len(shape) - 1)


def left_kernel(
    grads, errors, q_hbm, master, m_state, v_state,
    merged_hbm, part_ref, states_hbm,
    merged_ref, buffer, q_buffer, state_buffer, states_ref, sems, out_sems, small_sems,
):
    size = HALF // LEFT_CHUNKS
    small = [pltpu.make_async_copy(q_hbm, q_buffer, small_sems.at[0])]
    for n, source in enumerate((master, m_state, v_state)):
        small.append(pltpu.make_async_copy(source, state_buffer.at[n], small_sems.at[n + 1]))
    for copy in small:
        copy.start()
    copies = []
    for c in range(LEFT_CHUNKS):
        rows = pl.ds(c * size, size)
        pair = (
            pltpu.make_async_copy(grads.at[:, rows], merged_ref.at[:, rows], sems.at[0, c]),
            pltpu.make_async_copy(errors.at[:, rows], buffer.at[:, rows], sems.at[1, c]),
        )
        copies.append(pair)
    for copy in sum(copies[:AHEAD], ()):
        copy.start()
    small[0].wait()
    q = q_buffer[...]
    q_high = q.astype(bf16).astype(f32)
    right = jnp.concatenate([q_high, q - q_high], axis=0).T.astype(bf16)
    for n in range(3):
        small[n + 1].wait()
        states_ref[n] = state_buffer[n].astype(bf16)
    outs = [pltpu.make_async_copy(states_ref, states_hbm, small_sems.at[4])]
    outs[0].start()
    low_lanes = lanes((size, 2 * RANK)) < RANK
    for c in range(LEFT_CHUNKS):
        for copy in copies[c]:
            copy.wait()
        for copy in sum(copies[c + AHEAD : c + AHEAD + 1], ()):
            copy.start()
        rows = pl.ds(c * size, size)
        merged = merged_ref[:, rows] + buffer[:, rows]
        merged_ref[:, rows] = merged
        outs.append(
            pltpu.make_async_copy(merged_ref.at[:, rows], merged_hbm.at[:, rows], out_sems.at[c])
        )
        outs[-1].start()
        part = dot(merged.reshape(2 * size, COLS).astype(bf16), right, 1, 0)
        part = part + pltpu.roll(part, RANK, 1)
        part_ref[rows, :] = jnp.where(low_lanes, part[:size], part[size:]).astype(bf16)
    for copy in outs:
        copy.wait()


def left(grads, errors, q_init, master, m_state, v_state):
    return pl.pallas_call(
        left_kernel,
        out_shape=(
            pltpu.HBM((2, HALF, COLS), f32),
            jax.ShapeDtypeStruct((HALF, 2 * RANK), bf16),
            pltpu.HBM((3, ROWS, COLS), bf16),
        ),
        in_specs=[pl.BlockSpec(memory_space=pltpu.HBM)] * 6,
        out_specs=(
            pl.BlockSpec(memory_space=pltpu.HBM),
            pl.BlockSpec(memory_space=pltpu.VMEM),
            pl.BlockSpec(memory_space=pltpu.HBM),
        ),
        scratch_shapes=[
            pltpu.VMEM((2, HALF, COLS), f32),
            pltpu.VMEM((2, HALF, COLS), f32),
            pltpu.VMEM((RANK, COLS), f32),
            pltpu.VMEM((3, ROWS, COLS), f32),
            pltpu.VMEM((3, ROWS, COLS), bf16),
            pltpu.SemaphoreType.DMA((2, LEFT_CHUNKS)),
            pltpu.SemaphoreType.DMA((LEFT_CHUNKS,)),
            pltpu.SemaphoreType.DMA((5,)),
        ],
        compiler_params=pltpu.CompilerParams(vmem_limit_bytes=20 * MIB),
        name="left_factor",
    )(
        hbm(grads.reshape(2, HALF, COLS)), hbm(errors.reshape(2, HALF, COLS)), hbm(q_init.T),
        hbm(master), hbm(m_state), hbm(v_state),
    )


def sum_kernel(parts_ref, out_ref):
    total = jnp.sum(parts_ref[...].astype(f32).reshape(out_ref.shape), axis=0, keepdims=True)
    out_ref[...] = jnp.broadcast_to(total, out_ref.shape)


def sum_repeat(parts):
    return pl.pallas_call(
        sum_kernel,
        out_shape=jax.ShapeDtypeStruct((128, 8, 128), f32),
        in_specs=[pl.BlockSpec(memory_space=pltpu.VMEM)],
        out_specs=pl.BlockSpec(memory_space=pltpu.VMEM),
        compiler_params=pltpu.CompilerParams(vmem_limit_bytes=16 * MIB),
        name="sum_repeat",
    )(parts)


def inverse_factor(gram, after_panel):
    row_id = lax.broadcasted_iota(jnp.int32, (RANK, 2 * RANK), 0)
    lane = lanes((RANK, 2 * RANK))
    eye = jnp.where(row_id == lane, 1.0, 0.0).astype(f32)
    trace = jnp.sum(gram * eye, keepdims=True)
    jitter = 1e-06 * trace / RANK + 1e-06
    start = jnp.where(lane < RANK, gram + jitter * eye, jnp.where(row_id == lane - RANK, 1.0, 0.0))
    count = RANK // 8
    tiles = [start[8 * k : 8 * k + 8] for k in range(count)]
    sub = lax.broadcasted_iota(jnp.int32, (8, 2 * RANK), 0)
    for t in range(count):
        below = range(t, count)
        columns = {
            (c, k): jnp.broadcast_to(tiles[k][:, 8 * t + c : 8 * t + c + 1], sub.shape)
            for c in range(8)
            for k in below
        }
        for c in range(8):
            reciprocal = 1.0 / columns[c, t][c : c + 1]
            factors = {k: columns[c, k] * reciprocal for k in below}
            factors[t] = jnp.where(sub > c, factors[t], 0.0)
            for later in range(c + 1, 8):
                pivot_row = columns[later, t][c : c + 1]
                for k in below:
                    columns[later, k] = columns[later, k] - factors[k] * pivot_row
            pivot_row = tiles[t][c : c + 1]
            for k in below:
                tiles[k] = tiles[k] - factors[k] * pivot_row
        after_panel(t)
    done = jnp.concatenate(tiles, axis=0)
    pivots = jnp.sum(done * eye, axis=1, keepdims=True)
    return jnp.where(lane < RANK, 0.0, done * (1.0 / jnp.sqrt(pivots)))


def pair_rows(packed):
    low_lanes = lanes(packed.shape) < RANK
    high = packed.astype(bf16).astype(f32)
    low = packed - high
    top = jnp.where(low_lanes, high, pltpu.roll(low, RANK, 1)).astype(bf16)
    bottom = jnp.where(low_lanes, pltpu.roll(high, RANK, 1), low).astype(bf16)
    return top, bottom


def pair_gram(halves):
    square = sum(dot(half, half, 0, 0) for half in halves)
    square = square[:RANK] + square[RANK:]
    return square + pltpu.roll(square, RANK, 1)


def right_kernel(p_ref, merged_hbm, orth_ref, square_ref, part_ref, merged_ref, sems):
    def copy(c):
        half, rows = c // 4, pl.ds(c % 4 * BLOCK, BLOCK)
        return pltpu.make_async_copy(
            merged_hbm.at[half, rows], merged_ref.at[half, rows], sems.at[c]
        )

    for c in range(AHEAD):
        copy(c).start()
    pairs = pair_rows(p_ref[...])
    acc = [jnp.zeros((2 * RANK, COLS), f32)]

    def multiply(c):
        copy(c).wait()
        if c + AHEAD < D // BLOCK:
            copy(c + AHEAD).start()
        half, rows = c // 4, pl.ds(c % 4 * BLOCK, BLOCK)
        left = pairs[half][c % 4 * BLOCK : (c % 4 + 1) * BLOCK]
        acc[0] = acc[0] + dot(left, merged_ref[half, rows].astype(bf16), 0, 0)

    inverse = inverse_factor(pair_gram(pairs), multiply)
    part = acc[0][:RANK] + acc[0][RANK:]

    flipped = pltpu.roll(inverse, RANK, 1)
    inverse_small = flipped[:, :RANK]
    part_ref[...] = (dot(inverse_small, part, 1, 0, HIGHEST) * (1.0 / REPLICAS)).astype(bf16)

    high = inverse_small.astype(bf16).astype(f32)
    factor = jnp.concatenate([high, inverse_small - high], axis=0).T
    factor = jnp.concatenate([factor, factor], axis=0).astype(bf16)
    halves = []
    low_lanes = lanes((HALF, 2 * RANK)) < RANK
    for half in range(2):
        orth = dot(pairs[half], factor, 1, 0)
        orth = orth + pltpu.roll(orth, RANK, 1)
        high = orth.astype(bf16).astype(f32)
        pair = jnp.where(low_lanes, high, orth - high).astype(bf16)
        orth_ref[half * HALF : (half + 1) * HALF] = pair
        halves.append(pair)
    square_ref[...] = pair_gram(halves)


def right(packed, merged):
    return pl.pallas_call(
        right_kernel,
        out_shape=(
            jax.ShapeDtypeStruct((D, 2 * RANK), bf16),
            jax.ShapeDtypeStruct((RANK, 2 * RANK), f32),
            jax.ShapeDtypeStruct((RANK, COLS), bf16),
        ),
        in_specs=[
            pl.BlockSpec(memory_space=pltpu.VMEM),
            pl.BlockSpec(memory_space=pltpu.HBM),
        ],
        out_specs=(pl.BlockSpec(memory_space=pltpu.VMEM),) * 3,
        scratch_shapes=[
            pltpu.VMEM((2, HALF, COLS), f32),
            pltpu.SemaphoreType.DMA((D // BLOCK,)),
        ],
        compiler_params=pltpu.CompilerParams(vmem_limit_bytes=16 * MIB),
        name="right_factor",
    )(packed, hbm(merged))


def adam(update, master, m_state, v_state):
    m_new = beta_first * m_state + (1.0 - beta_first) * update
    v_new = beta_second * v_state + (1.0 - beta_second) * update * update
    m_hat = m_new / (1.0 - beta_first**STEP)
    v_hat = v_new / (1.0 - beta_second**STEP)
    master_new = master * (1.0 - learning_rate * decay_weight) - learning_rate * m_hat / (
        jnp.sqrt(v_hat) + adam_eps
    )
    return m_new, v_new, master_new


def new_weights(update, master, m_state, v_state):
    first = learning_rate / (1.0 - beta_first**STEP)
    second = 1.0 / (1.0 - beta_second**STEP)
    top = (first * beta_first) * m_state + (first * (1.0 - beta_first)) * update
    square = (second * beta_second) * v_state + (second * (1.0 - beta_second)) * (update * update)
    root = square * lax.rsqrt(square) + adam_eps
    return (1.0 - learning_rate * decay_weight) * master - top * pl.reciprocal(root, approx=True)


def final_kernel(
    q_ref, orth_ref, square_ref, merged_hbm, states_hbm, master_ref, m_ref, v_ref,
    error_hbm, weights_hbm, q_hbm, master_hbm, m_hbm, v_hbm,
    states_ref, merged_ref, error_ref, weights_ref, q_out, owned_ref, both_ref,
    in_sems, merged_sems, error_sems, weight_sems, small_sems,
):
    steps = D // BLOCK
    per = BLOCK // ROWS

    def states_copy(c):
        part = pl.ds(c * per, per)
        return pltpu.make_async_copy(states_hbm.at[part], states_ref.at[part], in_sems.at[c])

    def merged_copy(c):
        half = c // (steps // 2)
        rows = pl.ds(pl.multiple_of((c - half * (steps // 2)) * BLOCK, BLOCK), BLOCK)
        whole = pl.ds(pl.multiple_of(c * BLOCK, BLOCK), BLOCK)
        return pltpu.make_async_copy(
            merged_hbm.at[half, rows], merged_ref.at[whole], merged_sems.at[c]
        )

    def out_copies(c):
        rows = pl.ds(pl.multiple_of(c * BLOCK, BLOCK), BLOCK)
        return (
            pltpu.make_async_copy(error_ref.at[rows], error_hbm.at[rows], error_sems.at[c]),
            pltpu.make_async_copy(weights_ref.at[rows], weights_hbm.at[rows], weight_sems.at[c]),
        )

    for c in range(AHEAD):
        merged_copy(c).start()
        states_copy(c).start()
    gram = jnp.zeros((RANK, RANK), f32)
    for z in range(4):
        gram = gram + dot(q_ref[z], q_ref[z], 1, 1)
    total = jnp.sum(gram * square_ref[:, :RANK], keepdims=True)
    scale = 1.0 / jnp.sqrt(total / (D * HID) + norm_eps)
    q = q_ref[lax.axis_index("mp")]
    both_ref[:RANK] = q
    both_ref[RANK:] = q
    q_out[...] = q.astype(f32)
    start = pl.multiple_of(lax.axis_index("dp") * ROWS, ROWS)
    decoded = dot(orth_ref[pl.ds(start, ROWS)], both_ref[...], 1, 0)
    owned = adam(decoded * scale, master_ref[...], m_ref[...], v_ref[...])
    small = [pltpu.make_async_copy(q_out, q_hbm, small_sems.at[3])]
    for n, target in enumerate((m_hbm, v_hbm, master_hbm)):
        owned_ref[n] = owned[n]
        small.append(pltpu.make_async_copy(owned_ref.at[n], target, small_sems.at[n]))
    for copy in small:
        copy.start()

    @pl.loop(0, steps)
    def _(c):
        rows = pl.ds(pl.multiple_of(c * BLOCK, BLOCK), BLOCK)
        decoded = dot(orth_ref[rows], both_ref[...], 1, 0)
        merged_copy(c).wait()

        @pl.when(c + AHEAD < steps)
        def _():
            merged_copy(c + AHEAD).start()
            states_copy(c + AHEAD).start()

        error_ref[rows] = merged_ref[rows] - decoded
        update = decoded * scale
        states_copy(c).wait()
        for k in range(per):
            state = [states_ref[c * per + k, n].astype(f32) for n in range(3)]
            block = pl.ds(pl.multiple_of(c * BLOCK + k * ROWS, ROWS), ROWS)
            weights_ref[block] = new_weights(update[k * ROWS : (k + 1) * ROWS], *state).astype(bf16)
        for copy in out_copies(c):
            copy.start()

    for c in range(steps):
        for copy in out_copies(c):
            copy.wait()
    for copy in small:
        copy.wait()


def final(q_all, orth, square, merged, states, master, m_state, v_state):
    steps = D // BLOCK
    return pl.pallas_call(
        final_kernel,
        out_shape=(
            jax.ShapeDtypeStruct((D, COLS), f32),
            jax.ShapeDtypeStruct((D, COLS), bf16),
            jax.ShapeDtypeStruct((RANK, COLS), f32),
            jax.ShapeDtypeStruct((ROWS, COLS), f32),
            jax.ShapeDtypeStruct((ROWS, COLS), f32),
            jax.ShapeDtypeStruct((ROWS, COLS), f32),
        ),
        in_specs=[pl.BlockSpec(memory_space=pltpu.VMEM)] * 3
        + [pl.BlockSpec(memory_space=pltpu.HBM)] * 2
        + [pl.BlockSpec(memory_space=pltpu.VMEM)] * 3,
        out_specs=(pl.BlockSpec(memory_space=pl.ANY),) * 6,
        scratch_shapes=[
            pltpu.VMEM((REPLICAS, 3, ROWS, COLS), bf16),
            pltpu.VMEM((D, COLS), f32),
            pltpu.VMEM((D, COLS), f32),
            pltpu.VMEM((D, COLS), bf16),
            pltpu.VMEM((RANK, COLS), f32),
            pltpu.VMEM((3, ROWS, COLS), f32),
            pltpu.VMEM((2 * RANK, COLS), bf16),
            pltpu.SemaphoreType.DMA((steps,)),
            pltpu.SemaphoreType.DMA((steps,)),
            pltpu.SemaphoreType.DMA((steps,)),
            pltpu.SemaphoreType.DMA((steps,)),
            pltpu.SemaphoreType.DMA((4,)),
        ],
        compiler_params=pltpu.CompilerParams(vmem_limit_bytes=32 * MIB),
        name="decode_update",
    )(q_all, orth, square, hbm(merged), hbm(states), master, m_state, v_state)


def shards(grads, errors, q_init, master, m_state, v_state):
    merged, part, states = left(grads, errors, q_init, master, m_state, v_state)
    states = lax.all_gather(states, "dp", axis=0, tiled=False)
    parts = lax.all_to_all(part.reshape(128, 8, 128), ("dp", "mp"), 0, 0)
    owned = sum_repeat(parts.reshape(HALF, 128))
    packed = lax.all_to_all(owned, ("dp", "mp"), 0, 0).reshape(HALF, 128)
    orth, square, q_part = right(packed, merged)
    q_parts = lax.all_to_all(q_part.reshape(32, 2, COLS), "dp", 0, 0)
    q_owned = jnp.sum(q_parts.astype(f32), axis=0).astype(bf16)
    q_owned = jnp.broadcast_to(q_owned[None], (128, 2, COLS))
    q_all = lax.all_to_all(q_owned, ("mp", "dp"), 0, 0).reshape(4, RANK, COLS)
    error_new, weights, q_new, master_new, m_new, v_new = final(
        q_all, orth, square, merged, states, master, m_state, v_state
    )
    return (error_new[None], q_new.T, master_new, m_new, v_new, weights)


def solution(mesh):
    in_specs = (
        P("dp", None, "mp"),
        P("dp", None, "mp"),
        P("mp", None),
        P("dp", "mp"),
        P("dp", "mp"),
        P("dp", "mp"),
    )
    out_specs = (
        P("dp", None, "mp"),
        P("mp", None),
        P("dp", "mp"),
        P("dp", "mp"),
        P("dp", "mp"),
        P(None, "mp"),
    )
    return jax.shard_map(shards, mesh=mesh, in_specs=in_specs, out_specs=out_specs, check_vma=False)
```

```python
import jax
import jax.numpy as jnp
from jax import lax
from jax.experimental import pallas as pl
from jax.experimental.pallas import tpu as pltpu
from jax.sharding import PartitionSpec as P

D = 2048
HID = 2560
STEP = 100
RANK = 64
REPLICAS = 32
HALF = D // 2
COLS = 640
ROWS = 64

beta_first = 0.9
beta_second = 0.95
learning_rate = 0.01
decay_weight = 0.1
adam_eps = 1e-08
norm_eps = 1e-06

f32 = jnp.float32
bf16 = jnp.bfloat16
HIGHEST = lax.Precision.HIGHEST
MIB = 1024 * 1024
LEFT_CHUNKS = 8
AHEAD = 5
DELAY = 2
RIGHT_AHEAD = 3
BLOCK = 256


def dot(a, b, ca, cb, precision=None):
    return lax.dot_general(
        a, b, (((ca,), (cb,)), ((), ())), precision=precision, preferred_element_type=f32
    )


def hbm(x):
    return pltpu.with_memory_space_constraint(x, pltpu.HBM)


def lanes(shape):
    return lax.broadcasted_iota(jnp.int32, shape, len(shape) - 1)


def left_kernel(
    grads, errors, q_hbm, master, m_state, v_state,
    merged_hbm, part_ref, states_hbm,
    merged_ref, buffer, q_buffer, state_buffer, states_ref, sems, out_sems, small_sems,
):
    size = HALF // LEFT_CHUNKS
    small = [pltpu.make_async_copy(q_hbm, q_buffer, small_sems.at[0])]
    for n, source in enumerate((master, m_state, v_state)):
        small.append(pltpu.make_async_copy(source, state_buffer.at[n], small_sems.at[n + 1]))
    small[0].start()
    copies = []
    for c in range(LEFT_CHUNKS):
        rows = pl.ds(c * size, size)
        pair = (
            pltpu.make_async_copy(grads.at[:, rows], merged_ref.at[:, rows], sems.at[0, c]),
            pltpu.make_async_copy(errors.at[:, rows], buffer.at[:, rows], sems.at[1, c]),
        )
        for copy in pair:
            copy.start()
        copies.append(pair)
    for copy in small[1:]:
        copy.start()
    low_lanes = lanes((size, 2 * RANK)) < RANK
    outs = []
    right = None
    for c in range(LEFT_CHUNKS + DELAY):
        if c < LEFT_CHUNKS:
            rows = pl.ds(c * size, size)
            for copy in copies[c]:
                copy.wait()
            merged_ref[:, rows] = merged_ref[:, rows] + buffer[:, rows]
            outs.append(
                pltpu.make_async_copy(
                    merged_ref.at[:, rows], merged_hbm.at[:, rows], out_sems.at[c]
                )
            )
            outs[-1].start()
        if c == DELAY:
            small[0].wait()
            q = q_buffer[...]
            q_high = q.astype(bf16).astype(f32)
            right = jnp.concatenate([q_high, q - q_high], axis=0).T.astype(bf16)
        if c == LEFT_CHUNKS - 1:
            for n in range(3):
                small[n + 1].wait()
                states_ref[n] = state_buffer[n].astype(bf16)
            outs.append(pltpu.make_async_copy(states_ref, states_hbm, small_sems.at[4]))
            outs[-1].start()
        if c >= DELAY:
            rows = pl.ds((c - DELAY) * size, size)
            merged = merged_ref[:, rows].reshape(2 * size, COLS).astype(bf16)
            part = dot(merged, right, 1, 0)
            part = part + pltpu.roll(part, RANK, 1)
            part_ref[rows, :] = jnp.where(low_lanes, part[:size], part[size:]).astype(bf16)
    for copy in outs:
        copy.wait()


def left(grads, errors, q_init, master, m_state, v_state):
    return pl.pallas_call(
        left_kernel,
        out_shape=(
            pltpu.HBM((2, HALF, COLS), f32),
            jax.ShapeDtypeStruct((HALF, 2 * RANK), bf16),
            pltpu.HBM((3, ROWS, COLS), bf16),
        ),
        in_specs=[pl.BlockSpec(memory_space=pltpu.HBM)] * 6,
        out_specs=(
            pl.BlockSpec(memory_space=pltpu.HBM),
            pl.BlockSpec(memory_space=pltpu.VMEM),
            pl.BlockSpec(memory_space=pltpu.HBM),
        ),
        scratch_shapes=[
            pltpu.VMEM((2, HALF, COLS), f32),
            pltpu.VMEM((2, HALF, COLS), f32),
            pltpu.VMEM((RANK, COLS), f32),
            pltpu.VMEM((3, ROWS, COLS), f32),
            pltpu.VMEM((3, ROWS, COLS), bf16),
            pltpu.SemaphoreType.DMA((2, LEFT_CHUNKS)),
            pltpu.SemaphoreType.DMA((LEFT_CHUNKS,)),
            pltpu.SemaphoreType.DMA((5,)),
        ],
        compiler_params=pltpu.CompilerParams(vmem_limit_bytes=20 * MIB),
        name="left_factor",
    )(
        hbm(grads.reshape(2, HALF, COLS)), hbm(errors.reshape(2, HALF, COLS)), hbm(q_init.T),
        hbm(master), hbm(m_state), hbm(v_state),
    )


def sum_kernel(parts_ref, out_ref):
    total = jnp.sum(parts_ref[...].astype(f32).reshape(out_ref.shape), axis=0, keepdims=True)
    out_ref[...] = jnp.broadcast_to(total, out_ref.shape)


def sum_repeat(parts):
    return pl.pallas_call(
        sum_kernel,
        out_shape=jax.ShapeDtypeStruct((128, 8, 128), f32),
        in_specs=[pl.BlockSpec(memory_space=pltpu.VMEM)],
        out_specs=pl.BlockSpec(memory_space=pltpu.VMEM),
        compiler_params=pltpu.CompilerParams(vmem_limit_bytes=16 * MIB),
        name="sum_repeat",
    )(parts)


def inverse_factor(gram, after_panel):
    row_id = lax.broadcasted_iota(jnp.int32, (RANK, 2 * RANK), 0)
    lane = lanes((RANK, 2 * RANK))
    eye = jnp.where(row_id == lane, 1.0, 0.0).astype(f32)
    trace = jnp.sum(gram * eye, keepdims=True)
    jitter = 1e-06 * trace / RANK + 1e-06
    start = jnp.where(lane < RANK, gram + jitter * eye, jnp.where(row_id == lane - RANK, 1.0, 0.0))
    count = RANK // 8
    tiles = [start[8 * k : 8 * k + 8] for k in range(count)]
    sub = lax.broadcasted_iota(jnp.int32, (8, 2 * RANK), 0)
    for t in range(count):
        below = range(t, count)
        columns = {
            (c, k): jnp.broadcast_to(tiles[k][:, 8 * t + c : 8 * t + c + 1], sub.shape)
            for c in range(8)
            for k in below
        }
        for c in range(8):
            reciprocal = 1.0 / columns[c, t][c : c + 1]
            factors = {k: columns[c, k] * reciprocal for k in below}
            factors[t] = jnp.where(sub > c, factors[t], 0.0)
            for later in range(c + 1, 8):
                pivot_row = columns[later, t][c : c + 1]
                for k in below:
                    columns[later, k] = columns[later, k] - factors[k] * pivot_row
            pivot_row = tiles[t][c : c + 1]
            for k in below:
                tiles[k] = tiles[k] - factors[k] * pivot_row
        after_panel(t)
    done = jnp.concatenate(tiles, axis=0)
    pivots = jnp.sum(done * eye, axis=1, keepdims=True)
    return jnp.where(lane < RANK, 0.0, done * (1.0 / jnp.sqrt(pivots)))


def pair_rows(packed):
    low_lanes = lanes(packed.shape) < RANK
    high = packed.astype(bf16).astype(f32)
    low = packed - high
    top = jnp.where(low_lanes, high, pltpu.roll(low, RANK, 1)).astype(bf16)
    bottom = jnp.where(low_lanes, pltpu.roll(high, RANK, 1), low).astype(bf16)
    return top, bottom


def pair_gram(halves):
    square = sum(dot(half, half, 0, 0) for half in halves)
    square = square[:RANK] + square[RANK:]
    return square + pltpu.roll(square, RANK, 1)


def right_kernel(p_ref, merged_hbm, orth_ref, square_ref, part_ref, merged_ref, sems):
    def copy(c):
        half, rows = c // 4, pl.ds(c % 4 * BLOCK, BLOCK)
        return pltpu.make_async_copy(
            merged_hbm.at[half, rows], merged_ref.at[half, rows], sems.at[c]
        )

    for c in range(RIGHT_AHEAD):
        copy(c).start()
    pairs = pair_rows(p_ref[...])
    acc = [jnp.zeros((2 * RANK, COLS), f32)]

    def multiply(c):
        copy(c).wait()
        if c + RIGHT_AHEAD < D // BLOCK:
            copy(c + RIGHT_AHEAD).start()
        half, rows = c // 4, pl.ds(c % 4 * BLOCK, BLOCK)
        left = pairs[half][c % 4 * BLOCK : (c % 4 + 1) * BLOCK]
        acc[0] = acc[0] + dot(left, merged_ref[half, rows].astype(bf16), 0, 0)

    inverse = inverse_factor(pair_gram(pairs), multiply)
    part = acc[0][:RANK] + acc[0][RANK:]

    flipped = pltpu.roll(inverse, RANK, 1)
    inverse_small = flipped[:, :RANK]
    part_ref[...] = (dot(inverse_small, part, 1, 0, HIGHEST) * (1.0 / REPLICAS)).astype(bf16)

    high = inverse_small.astype(bf16).astype(f32)
    factor = jnp.concatenate([high, inverse_small - high], axis=0).T
    factor = jnp.concatenate([factor, factor], axis=0).astype(bf16)
    halves = []
    low_lanes = lanes((HALF, 2 * RANK)) < RANK
    for half in range(2):
        orth = dot(pairs[half], factor, 1, 0)
        orth = orth + pltpu.roll(orth, RANK, 1)
        high = orth.astype(bf16).astype(f32)
        pair = jnp.where(low_lanes, high, orth - high).astype(bf16)
        orth_ref[half * HALF : (half + 1) * HALF] = pair
        halves.append(pair)
    square_ref[...] = pair_gram(halves)


def right(packed, merged):
    return pl.pallas_call(
        right_kernel,
        out_shape=(
            jax.ShapeDtypeStruct((D, 2 * RANK), bf16),
            jax.ShapeDtypeStruct((RANK, 2 * RANK), f32),
            jax.ShapeDtypeStruct((RANK, COLS), bf16),
        ),
        in_specs=[
            pl.BlockSpec(memory_space=pltpu.VMEM),
            pl.BlockSpec(memory_space=pltpu.HBM),
        ],
        out_specs=(pl.BlockSpec(memory_space=pltpu.VMEM),) * 3,
        scratch_shapes=[
            pltpu.VMEM((2, HALF, COLS), f32),
            pltpu.SemaphoreType.DMA((D // BLOCK,)),
        ],
        compiler_params=pltpu.CompilerParams(vmem_limit_bytes=16 * MIB),
        name="right_factor",
    )(packed, hbm(merged))


def adam(update, master, m_state, v_state):
    m_new = beta_first * m_state + (1.0 - beta_first) * update
    v_new = beta_second * v_state + (1.0 - beta_second) * update * update
    m_hat = m_new / (1.0 - beta_first**STEP)
    v_hat = v_new / (1.0 - beta_second**STEP)
    master_new = master * (1.0 - learning_rate * decay_weight) - learning_rate * m_hat / (
        jnp.sqrt(v_hat) + adam_eps
    )
    return m_new, v_new, master_new


def new_weights(update, master, m_state, v_state):
    first = learning_rate / (1.0 - beta_first**STEP)
    second = 1.0 / (1.0 - beta_second**STEP)
    top = (first * beta_first) * m_state + (first * (1.0 - beta_first)) * update
    square = (second * beta_second) * v_state + (second * (1.0 - beta_second)) * (update * update)
    root = square * lax.rsqrt(square) + adam_eps
    return (1.0 - learning_rate * decay_weight) * master - top * pl.reciprocal(root, approx=True)


def final_kernel(
    q_ref, orth_ref, square_ref, merged_hbm, states_hbm, master_ref, m_ref, v_ref,
    error_hbm, weights_hbm, q_hbm, master_hbm, m_hbm, v_hbm,
    states_ref, merged_ref, error_ref, weights_ref, q_out, owned_ref, both_ref,
    in_sems, merged_sems, error_sems, weight_sems, small_sems,
):
    steps = D // BLOCK
    per = BLOCK // ROWS

    def states_copy(c):
        part = pl.ds(c * per, per)
        return pltpu.make_async_copy(states_hbm.at[part], states_ref.at[part], in_sems.at[c])

    def merged_copy(c):
        half = c // (steps // 2)
        rows = pl.ds(pl.multiple_of((c - half * (steps // 2)) * BLOCK, BLOCK), BLOCK)
        whole = pl.ds(pl.multiple_of(c * BLOCK, BLOCK), BLOCK)
        return pltpu.make_async_copy(
            merged_hbm.at[half, rows], merged_ref.at[whole], merged_sems.at[c]
        )

    def out_copies(c):
        rows = pl.ds(pl.multiple_of(c * BLOCK, BLOCK), BLOCK)
        return (
            pltpu.make_async_copy(error_ref.at[rows], error_hbm.at[rows], error_sems.at[c]),
            pltpu.make_async_copy(weights_ref.at[rows], weights_hbm.at[rows], weight_sems.at[c]),
        )

    for c in range(AHEAD):
        merged_copy(c).start()
        states_copy(c).start()
    gram = jnp.zeros((RANK, RANK), f32)
    for z in range(4):
        gram = gram + dot(q_ref[z], q_ref[z], 1, 1)
    total = jnp.sum(gram * square_ref[:, :RANK], keepdims=True)
    scale = 1.0 / jnp.sqrt(total / (D * HID) + norm_eps)
    q = q_ref[lax.axis_index("mp")]
    both_ref[:RANK] = q
    both_ref[RANK:] = q
    q_out[...] = q.astype(f32)
    start = pl.multiple_of(lax.axis_index("dp") * ROWS, ROWS)
    decoded = dot(orth_ref[pl.ds(start, ROWS)], both_ref[...], 1, 0)
    owned = adam(decoded * scale, master_ref[...], m_ref[...], v_ref[...])
    small = [pltpu.make_async_copy(q_out, q_hbm, small_sems.at[3])]
    for n, target in enumerate((m_hbm, v_hbm, master_hbm)):
        owned_ref[n] = owned[n]
        small.append(pltpu.make_async_copy(owned_ref.at[n], target, small_sems.at[n]))
    for copy in small:
        copy.start()

    @pl.loop(0, steps)
    def _(c):
        rows = pl.ds(pl.multiple_of(c * BLOCK, BLOCK), BLOCK)
        decoded = dot(orth_ref[rows], both_ref[...], 1, 0)
        merged_copy(c).wait()

        @pl.when(c + AHEAD < steps)
        def _():
            merged_copy(c + AHEAD).start()
            states_copy(c + AHEAD).start()

        error_ref[rows] = merged_ref[rows] - decoded
        update = decoded * scale
        states_copy(c).wait()
        for k in range(per):
            state = [states_ref[c * per + k, n].astype(f32) for n in range(3)]
            block = pl.ds(pl.multiple_of(c * BLOCK + k * ROWS, ROWS), ROWS)
            weights_ref[block] = new_weights(update[k * ROWS : (k + 1) * ROWS], *state).astype(bf16)
        for copy in out_copies(c):
            copy.start()

    for c in range(steps):
        for copy in out_copies(c):
            copy.wait()
    for copy in small:
        copy.wait()


def final(q_all, orth, square, merged, states, master, m_state, v_state):
    steps = D // BLOCK
    return pl.pallas_call(
        final_kernel,
        out_shape=(
            jax.ShapeDtypeStruct((D, COLS), f32),
            jax.ShapeDtypeStruct((D, COLS), bf16),
            jax.ShapeDtypeStruct((RANK, COLS), f32),
            jax.ShapeDtypeStruct((ROWS, COLS), f32),
            jax.ShapeDtypeStruct((ROWS, COLS), f32),
            jax.ShapeDtypeStruct((ROWS, COLS), f32),
        ),
        in_specs=[pl.BlockSpec(memory_space=pltpu.VMEM)] * 3
        + [pl.BlockSpec(memory_space=pltpu.HBM)] * 2
        + [pl.BlockSpec(memory_space=pltpu.VMEM)] * 3,
        out_specs=(pl.BlockSpec(memory_space=pl.ANY),) * 6,
        scratch_shapes=[
            pltpu.VMEM((REPLICAS, 3, ROWS, COLS), bf16),
            pltpu.VMEM((D, COLS), f32),
            pltpu.VMEM((D, COLS), f32),
            pltpu.VMEM((D, COLS), bf16),
            pltpu.VMEM((RANK, COLS), f32),
            pltpu.VMEM((3, ROWS, COLS), f32),
            pltpu.VMEM((2 * RANK, COLS), bf16),
            pltpu.SemaphoreType.DMA((steps,)),
            pltpu.SemaphoreType.DMA((steps,)),
            pltpu.SemaphoreType.DMA((steps,)),
            pltpu.SemaphoreType.DMA((steps,)),
            pltpu.SemaphoreType.DMA((4,)),
        ],
        compiler_params=pltpu.CompilerParams(vmem_limit_bytes=32 * MIB),
        name="decode_update",
    )(q_all, orth, square, hbm(merged), hbm(states), master, m_state, v_state)


def shards(grads, errors, q_init, master, m_state, v_state):
    merged, part, states = left(grads, errors, q_init, master, m_state, v_state)
    states = lax.all_gather(states, "dp", axis=0, tiled=False)
    parts = lax.all_to_all(part.reshape(128, 8, 128), ("dp", "mp"), 0, 0)
    owned = sum_repeat(parts.reshape(HALF, 128))
    packed = lax.all_to_all(owned, ("dp", "mp"), 0, 0).reshape(HALF, 128)
    orth, square, q_part = right(packed, merged)
    q_parts = lax.all_to_all(q_part.reshape(32, 2, COLS), "dp", 0, 0)
    q_owned = jnp.sum(q_parts.astype(f32), axis=0).astype(bf16)
    q_owned = jnp.broadcast_to(q_owned[None], (128, 2, COLS))
    q_all = lax.all_to_all(q_owned, ("mp", "dp"), 0, 0).reshape(4, RANK, COLS)
    error_new, weights, q_new, master_new, m_new, v_new = final(
        q_all, orth, square, merged, states, master, m_state, v_state
    )
    return (error_new[None], q_new.T, master_new, m_new, v_new, weights)


def solution(mesh):
    in_specs = (
        P("dp", None, "mp"),
        P("dp", None, "mp"),
        P("mp", None),
        P("dp", "mp"),
        P("dp", "mp"),
        P("dp", "mp"),
    )
    out_specs = (
        P("dp", None, "mp"),
        P("mp", None),
        P("dp", "mp"),
        P("dp", "mp"),
        P("dp", "mp"),
        P(None, "mp"),
    )
    return jax.shard_map(shards, mesh=mesh, in_specs=in_specs, out_specs=out_specs, check_vma=False)
```

```python
import jax
import jax.numpy as jnp
from jax import lax
from jax.experimental import pallas as pl
from jax.experimental.pallas import tpu as pltpu
from jax.sharding import Mesh, PartitionSpec as P

D = 2048
HID = 2560
STEP = 100
RANK = 64
REPLICAS = 32
DP = ("y", "x", "c")
HALF = D // 2
COLS = 640
ROWS = 64

beta_first = 0.9
beta_second = 0.95
learning_rate = 0.01
decay_weight = 0.1
adam_eps = 1e-08
norm_eps = 1e-06

f32 = jnp.float32
bf16 = jnp.bfloat16
HIGHEST = lax.Precision.HIGHEST
MIB = 1024 * 1024
LEFT_CHUNKS = 8
AHEAD = 5
DELAY = 2
RIGHT_AHEAD = 3
BLOCK = 256


def dot(a, b, ca, cb, precision=None):
    return lax.dot_general(
        a, b, (((ca,), (cb,)), ((), ())), precision=precision, preferred_element_type=f32
    )


def hbm(x):
    return pltpu.with_memory_space_constraint(x, pltpu.HBM)


def lanes(shape):
    return lax.broadcasted_iota(jnp.int32, shape, len(shape) - 1)


def left_kernel(
    grads, errors, q_hbm, master, m_state, v_state,
    merged_hbm, part_ref, states_hbm,
    merged_ref, buffer, q_buffer, state_buffer, states_ref, sems, out_sems, small_sems,
):
    size = HALF // LEFT_CHUNKS
    small = [pltpu.make_async_copy(q_hbm, q_buffer, small_sems.at[0])]
    for n, source in enumerate((master, m_state, v_state)):
        small.append(pltpu.make_async_copy(source, state_buffer.at[n], small_sems.at[n + 1]))
    small[0].start()
    copies = []
    for c in range(LEFT_CHUNKS):
        rows = pl.ds(c * size, size)
        pair = (
            pltpu.make_async_copy(grads.at[:, rows], merged_ref.at[:, rows], sems.at[0, c]),
            pltpu.make_async_copy(errors.at[:, rows], buffer.at[:, rows], sems.at[1, c]),
        )
        for copy in pair:
            copy.start()
        copies.append(pair)
    for copy in small[1:]:
        copy.start()
    low_lanes = lanes((size, 2 * RANK)) < RANK
    outs = []
    right = None
    for c in range(LEFT_CHUNKS + DELAY):
        if c < LEFT_CHUNKS:
            rows = pl.ds(c * size, size)
            for copy in copies[c]:
                copy.wait()
            merged_ref[:, rows] = merged_ref[:, rows] + buffer[:, rows]
            outs.append(
                pltpu.make_async_copy(
                    merged_ref.at[:, rows], merged_hbm.at[:, rows], out_sems.at[c]
                )
            )
            outs[-1].start()
        if c == DELAY:
            small[0].wait()
            q = q_buffer[...]
            q_high = q.astype(bf16).astype(f32)
            right = jnp.concatenate([q_high, q - q_high], axis=0).T.astype(bf16)
        if c == LEFT_CHUNKS - 1:
            for n in range(3):
                small[n + 1].wait()
                states_ref[n] = state_buffer[n].astype(bf16)
            outs.append(pltpu.make_async_copy(states_ref, states_hbm, small_sems.at[4]))
            outs[-1].start()
        if c >= DELAY:
            rows = pl.ds((c - DELAY) * size, size)
            merged = merged_ref[:, rows].reshape(2 * size, COLS).astype(bf16)
            part = dot(merged, right, 1, 0)
            part = part + pltpu.roll(part, RANK, 1)
            part_ref[rows, :] = jnp.where(low_lanes, part[:size], part[size:]).astype(bf16)
    for copy in outs:
        copy.wait()


def left(grads, errors, q_init, master, m_state, v_state):
    return pl.pallas_call(
        left_kernel,
        out_shape=(
            pltpu.HBM((2, HALF, COLS), f32),
            jax.ShapeDtypeStruct((HALF, 2 * RANK), bf16),
            pltpu.HBM((3, ROWS, COLS), bf16),
        ),
        in_specs=[pl.BlockSpec(memory_space=pltpu.HBM)] * 6,
        out_specs=(
            pl.BlockSpec(memory_space=pltpu.HBM),
            pl.BlockSpec(memory_space=pltpu.VMEM),
            pl.BlockSpec(memory_space=pltpu.HBM),
        ),
        scratch_shapes=[
            pltpu.VMEM((2, HALF, COLS), f32),
            pltpu.VMEM((2, HALF, COLS), f32),
            pltpu.VMEM((RANK, COLS), f32),
            pltpu.VMEM((3, ROWS, COLS), f32),
            pltpu.VMEM((3, ROWS, COLS), bf16),
            pltpu.SemaphoreType.DMA((2, LEFT_CHUNKS)),
            pltpu.SemaphoreType.DMA((LEFT_CHUNKS,)),
            pltpu.SemaphoreType.DMA((5,)),
        ],
        compiler_params=pltpu.CompilerParams(vmem_limit_bytes=20 * MIB),
        name="left_factor",
    )(
        hbm(grads.reshape(2, HALF, COLS)), hbm(errors.reshape(2, HALF, COLS)), hbm(q_init.T),
        hbm(master), hbm(m_state), hbm(v_state),
    )


def sum_kernel(parts_ref, out_ref):
    total = jnp.sum(parts_ref[...].astype(f32).reshape(128, 8, 128), axis=0, keepdims=True)
    out_ref[...] = jnp.broadcast_to(total, out_ref.shape)


def sum_repeat(parts):
    return pl.pallas_call(
        sum_kernel,
        out_shape=jax.ShapeDtypeStruct((64, 8, 128), f32),
        in_specs=[pl.BlockSpec(memory_space=pltpu.VMEM)],
        out_specs=pl.BlockSpec(memory_space=pltpu.VMEM),
        compiler_params=pltpu.CompilerParams(vmem_limit_bytes=16 * MIB),
        name="sum_repeat",
    )(parts)


def inverse_factor(gram, after_panel):
    row_id = lax.broadcasted_iota(jnp.int32, (RANK, 2 * RANK), 0)
    lane = lanes((RANK, 2 * RANK))
    eye = jnp.where(row_id == lane, 1.0, 0.0).astype(f32)
    trace = jnp.sum(gram * eye, keepdims=True)
    jitter = 1e-06 * trace / RANK + 1e-06
    start = jnp.where(lane < RANK, gram + jitter * eye, jnp.where(row_id == lane - RANK, 1.0, 0.0))
    count = RANK // 8
    tiles = [start[8 * k : 8 * k + 8] for k in range(count)]
    sub = lax.broadcasted_iota(jnp.int32, (8, 2 * RANK), 0)
    for t in range(count):
        below = range(t, count)
        columns = {
            (c, k): jnp.broadcast_to(tiles[k][:, 8 * t + c : 8 * t + c + 1], sub.shape)
            for c in range(8)
            for k in below
        }
        for c in range(8):
            reciprocal = 1.0 / columns[c, t][c : c + 1]
            factors = {k: columns[c, k] * reciprocal for k in below}
            factors[t] = jnp.where(sub > c, factors[t], 0.0)
            for later in range(c + 1, 8):
                pivot_row = columns[later, t][c : c + 1]
                for k in below:
                    columns[later, k] = columns[later, k] - factors[k] * pivot_row
            pivot_row = tiles[t][c : c + 1]
            for k in below:
                tiles[k] = tiles[k] - factors[k] * pivot_row
        after_panel(t)
    done = jnp.concatenate(tiles, axis=0)
    pivots = jnp.sum(done * eye, axis=1, keepdims=True)
    return jnp.where(lane < RANK, 0.0, done * (1.0 / jnp.sqrt(pivots)))


def pair_rows(packed):
    low_lanes = lanes(packed.shape) < RANK
    high = packed.astype(bf16).astype(f32)
    low = packed - high
    top = jnp.where(low_lanes, high, pltpu.roll(low, RANK, 1)).astype(bf16)
    bottom = jnp.where(low_lanes, pltpu.roll(high, RANK, 1), low).astype(bf16)
    return top, bottom


def pair_gram(halves):
    square = sum(dot(half, half, 0, 0) for half in halves)
    square = square[:RANK] + square[RANK:]
    return square + pltpu.roll(square, RANK, 1)


def right_kernel(own_ref, other_ref, merged_hbm, orth_ref, square_ref, part_ref, merged_ref, sems):
    def copy(c):
        half, rows = c // 4, pl.ds(c % 4 * BLOCK, BLOCK)
        return pltpu.make_async_copy(
            merged_hbm.at[half, rows], merged_ref.at[half, rows], sems.at[c]
        )

    for c in range(RIGHT_AHEAD):
        copy(c).start()
    own, other = own_ref[...], other_ref[...]
    first = lax.axis_index("c") == 0
    packed = jnp.concatenate([jnp.where(first, own, other), jnp.where(first, other, own)], axis=0)
    pairs = pair_rows(packed)
    acc = [jnp.zeros((2 * RANK, COLS), f32)]

    def multiply(c):
        copy(c).wait()
        if c + RIGHT_AHEAD < D // BLOCK:
            copy(c + RIGHT_AHEAD).start()
        half, rows = c // 4, pl.ds(c % 4 * BLOCK, BLOCK)
        left = pairs[half][c % 4 * BLOCK : (c % 4 + 1) * BLOCK]
        acc[0] = acc[0] + dot(left, merged_ref[half, rows].astype(bf16), 0, 0)

    inverse = inverse_factor(pair_gram(pairs), multiply)
    part = acc[0][:RANK] + acc[0][RANK:]

    flipped = pltpu.roll(inverse, RANK, 1)
    inverse_small = flipped[:, :RANK]
    part_ref[...] = (dot(inverse_small, part, 1, 0, HIGHEST) * (1.0 / REPLICAS)).astype(bf16)

    high = inverse_small.astype(bf16).astype(f32)
    factor = jnp.concatenate([high, inverse_small - high], axis=0).T
    factor = jnp.concatenate([factor, factor], axis=0).astype(bf16)
    halves = []
    low_lanes = lanes((HALF, 2 * RANK)) < RANK
    for half in range(2):
        orth = dot(pairs[half], factor, 1, 0)
        orth = orth + pltpu.roll(orth, RANK, 1)
        high = orth.astype(bf16).astype(f32)
        pair = jnp.where(low_lanes, high, orth - high).astype(bf16)
        orth_ref[half * HALF : (half + 1) * HALF] = pair
        halves.append(pair)
    square_ref[...] = pair_gram(halves)


def right(own, other, merged):
    return pl.pallas_call(
        right_kernel,
        out_shape=(
            jax.ShapeDtypeStruct((D, 2 * RANK), bf16),
            jax.ShapeDtypeStruct((RANK, 2 * RANK), f32),
            jax.ShapeDtypeStruct((RANK, COLS), bf16),
        ),
        in_specs=[
            pl.BlockSpec(memory_space=pltpu.VMEM),
            pl.BlockSpec(memory_space=pltpu.VMEM),
            pl.BlockSpec(memory_space=pltpu.HBM),
        ],
        out_specs=(pl.BlockSpec(memory_space=pltpu.VMEM),) * 3,
        scratch_shapes=[
            pltpu.VMEM((2, HALF, COLS), f32),
            pltpu.SemaphoreType.DMA((D // BLOCK,)),
        ],
        compiler_params=pltpu.CompilerParams(vmem_limit_bytes=16 * MIB),
        name="right_factor",
    )(own, other, hbm(merged))


def adam(update, master, m_state, v_state):
    m_new = beta_first * m_state + (1.0 - beta_first) * update
    v_new = beta_second * v_state + (1.0 - beta_second) * update * update
    m_hat = m_new / (1.0 - beta_first**STEP)
    v_hat = v_new / (1.0 - beta_second**STEP)
    master_new = master * (1.0 - learning_rate * decay_weight) - learning_rate * m_hat / (
        jnp.sqrt(v_hat) + adam_eps
    )
    return m_new, v_new, master_new


def new_weights(update, master, m_state, v_state):
    first = learning_rate / (1.0 - beta_first**STEP)
    second = 1.0 / (1.0 - beta_second**STEP)
    top = (first * beta_first) * m_state + (first * (1.0 - beta_first)) * update
    square = (second * beta_second) * v_state + (second * (1.0 - beta_second)) * (update * update)
    root = square * lax.rsqrt(square) + adam_eps
    return (1.0 - learning_rate * decay_weight) * master - top * pl.reciprocal(root, approx=True)


def final_kernel(
    q_ref, orth_ref, square_ref, merged_hbm, states_hbm, master_ref, m_ref, v_ref,
    error_hbm, weights_hbm, q_hbm, master_hbm, m_hbm, v_hbm,
    states_ref, merged_ref, error_ref, weights_ref, q_out, owned_ref, both_ref,
    in_sems, merged_sems, error_sems, weight_sems, small_sems,
):
    steps = D // BLOCK
    per = BLOCK // ROWS

    def states_copy(c):
        part = pl.ds(c * per, per)
        return pltpu.make_async_copy(states_hbm.at[part], states_ref.at[part], in_sems.at[c])

    def merged_copy(c):
        half = c // (steps // 2)
        rows = pl.ds(pl.multiple_of((c - half * (steps // 2)) * BLOCK, BLOCK), BLOCK)
        whole = pl.ds(pl.multiple_of(c * BLOCK, BLOCK), BLOCK)
        return pltpu.make_async_copy(
            merged_hbm.at[half, rows], merged_ref.at[whole], merged_sems.at[c]
        )

    def out_copies(c):
        rows = pl.ds(pl.multiple_of(c * BLOCK, BLOCK), BLOCK)
        return (
            pltpu.make_async_copy(error_ref.at[rows], error_hbm.at[rows], error_sems.at[c]),
            pltpu.make_async_copy(weights_ref.at[rows], weights_hbm.at[rows], weight_sems.at[c]),
        )

    for c in range(AHEAD):
        merged_copy(c).start()
        states_copy(c).start()
    gram = jnp.zeros((RANK, RANK), f32)
    for z in range(4):
        gram = gram + dot(q_ref[z], q_ref[z], 1, 1)
    total = jnp.sum(gram * square_ref[:, :RANK], keepdims=True)
    scale = 1.0 / jnp.sqrt(total / (D * HID) + norm_eps)
    q = q_ref[lax.axis_index("z")]
    both_ref[:RANK] = q
    both_ref[RANK:] = q
    q_out[...] = q.astype(f32)
    start = pl.multiple_of(lax.axis_index(DP) * ROWS, ROWS)
    decoded = dot(orth_ref[pl.ds(start, ROWS)], both_ref[...], 1, 0)
    owned = adam(decoded * scale, master_ref[...], m_ref[...], v_ref[...])
    small = [pltpu.make_async_copy(q_out, q_hbm, small_sems.at[3])]
    for n, target in enumerate((m_hbm, v_hbm, master_hbm)):
        owned_ref[n] = owned[n]
        small.append(pltpu.make_async_copy(owned_ref.at[n], target, small_sems.at[n]))
    for copy in small:
        copy.start()

    @pl.loop(0, steps)
    def _(c):
        rows = pl.ds(pl.multiple_of(c * BLOCK, BLOCK), BLOCK)
        decoded = dot(orth_ref[rows], both_ref[...], 1, 0)
        merged_copy(c).wait()

        @pl.when(c + AHEAD < steps)
        def _():
            merged_copy(c + AHEAD).start()
            states_copy(c + AHEAD).start()

        error_ref[rows] = merged_ref[rows] - decoded
        update = decoded * scale
        states_copy(c).wait()
        for k in range(per):
            state = [states_ref[c * per + k, n].astype(f32) for n in range(3)]
            block = pl.ds(pl.multiple_of(c * BLOCK + k * ROWS, ROWS), ROWS)
            weights_ref[block] = new_weights(update[k * ROWS : (k + 1) * ROWS], *state).astype(bf16)
        for copy in out_copies(c):
            copy.start()

    for c in range(steps):
        for copy in out_copies(c):
            copy.wait()
    for copy in small:
        copy.wait()


def final(q_all, orth, square, merged, states, master, m_state, v_state):
    steps = D // BLOCK
    return pl.pallas_call(
        final_kernel,
        out_shape=(
            jax.ShapeDtypeStruct((D, COLS), f32),
            jax.ShapeDtypeStruct((D, COLS), bf16),
            jax.ShapeDtypeStruct((RANK, COLS), f32),
            jax.ShapeDtypeStruct((ROWS, COLS), f32),
            jax.ShapeDtypeStruct((ROWS, COLS), f32),
            jax.ShapeDtypeStruct((ROWS, COLS), f32),
        ),
        in_specs=[pl.BlockSpec(memory_space=pltpu.VMEM)] * 3
        + [pl.BlockSpec(memory_space=pltpu.HBM)] * 2
        + [pl.BlockSpec(memory_space=pltpu.VMEM)] * 3,
        out_specs=(pl.BlockSpec(memory_space=pl.ANY),) * 6,
        scratch_shapes=[
            pltpu.VMEM((REPLICAS, 3, ROWS, COLS), bf16),
            pltpu.VMEM((D, COLS), f32),
            pltpu.VMEM((D, COLS), f32),
            pltpu.VMEM((D, COLS), bf16),
            pltpu.VMEM((RANK, COLS), f32),
            pltpu.VMEM((3, ROWS, COLS), f32),
            pltpu.VMEM((2 * RANK, COLS), bf16),
            pltpu.SemaphoreType.DMA((steps,)),
            pltpu.SemaphoreType.DMA((steps,)),
            pltpu.SemaphoreType.DMA((steps,)),
            pltpu.SemaphoreType.DMA((steps,)),
            pltpu.SemaphoreType.DMA((4,)),
        ],
        compiler_params=pltpu.CompilerParams(vmem_limit_bytes=32 * MIB),
        name="decode_update",
    )(q_all, orth, square, hbm(merged), hbm(states), master, m_state, v_state)


def shards(grads, errors, q_init, master, m_state, v_state):
    merged, part, states = left(grads, errors, q_init, master, m_state, v_state)
    states = lax.all_gather(states, DP, axis=0, tiled=False)
    parts = lax.all_to_all(part.reshape(128, 8, 128), ("c", "y", "x", "z"), 0, 0)
    owned = sum_repeat(parts.reshape(HALF, 128))
    own = lax.all_to_all(owned, ("y", "x", "z"), 0, 0).reshape(HALF // 2, 128)
    other = lax.ppermute(own, "c", [(0, 1), (1, 0)])
    orth, square, q_part = right(own, other, merged)
    q_parts = lax.all_to_all(q_part.reshape(32, 2, COLS), DP, 0, 0)
    q_owned = jnp.sum(q_parts.astype(f32), axis=0).astype(bf16)
    q_owned = jnp.broadcast_to(q_owned[None], (128, 2, COLS))
    q_all = lax.all_to_all(q_owned, ("z",) + DP, 0, 0).reshape(4, RANK, COLS)
    error_new, weights, q_new, master_new, m_new, v_new = final(
        q_all, orth, square, merged, states, master, m_state, v_state
    )
    return (error_new[None], q_new.T, master_new, m_new, v_new, weights)


def solution(mesh):
    replicas, columns = mesh.devices.shape
    mesh = Mesh(mesh.devices.reshape(4, replicas // 8, 2, columns), DP + ("z",))
    in_specs = (
        P(DP, None, "z"),
        P(DP, None, "z"),
        P("z", None),
        P(DP, "z"),
        P(DP, "z"),
        P(DP, "z"),
    )
    out_specs = (
        P(DP, None, "z"),
        P("z", None),
        P(DP, "z"),
        P(DP, "z"),
        P(DP, "z"),
        P(None, "z"),
    )
    return jax.shard_map(shards, mesh=mesh, in_specs=in_specs, out_specs=out_specs, check_vma=False)
```

```python
import jax
import jax.numpy as jnp
from jax import lax
from jax.experimental import pallas as pl
from jax.experimental.pallas import tpu as pltpu
from jax.sharding import Mesh, PartitionSpec as P

D = 2048
HID = 2560
STEP = 100
RANK = 64
REPLICAS = 32
DP = ("y", "x", "c")
HALF = D // 2
COLS = 640
ROWS = 64

beta_first = 0.9
beta_second = 0.95
learning_rate = 0.01
decay_weight = 0.1
adam_eps = 1e-08
norm_eps = 1e-06

f32 = jnp.float32
bf16 = jnp.bfloat16
HIGHEST = lax.Precision.HIGHEST
MIB = 1024 * 1024
LEFT_CHUNKS = 8
AHEAD = 5
DELAY = 2
RIGHT_AHEAD = 4
BLOCK = 256


def dot(a, b, ca, cb, precision=None):
    return lax.dot_general(
        a, b, (((ca,), (cb,)), ((), ())), precision=precision, preferred_element_type=f32
    )


def hbm(x):
    return pltpu.with_memory_space_constraint(x, pltpu.HBM)


def lanes(shape):
    return lax.broadcasted_iota(jnp.int32, shape, len(shape) - 1)


def left_kernel(
    grads, errors, q_hbm, master, m_state, v_state,
    merged_hbm, part_ref, states_hbm,
    merged_ref, buffer, q_buffer, state_buffer, states_ref, sems, out_sems, small_sems,
):
    size = HALF // LEFT_CHUNKS
    small = [pltpu.make_async_copy(q_hbm, q_buffer, small_sems.at[0])]
    for n, source in enumerate((master, m_state, v_state)):
        small.append(pltpu.make_async_copy(source, state_buffer.at[n], small_sems.at[n + 1]))
    small[0].start()
    copies = []
    for c in range(LEFT_CHUNKS):
        rows = pl.ds(c * size, size)
        pair = (
            pltpu.make_async_copy(grads.at[:, rows], merged_ref.at[:, rows], sems.at[0, c]),
            pltpu.make_async_copy(errors.at[:, rows], buffer.at[:, rows], sems.at[1, c]),
        )
        for copy in pair:
            copy.start()
        copies.append(pair)
    for copy in small[1:]:
        copy.start()
    low_lanes = lanes((size, 2 * RANK)) < RANK
    outs = []
    right = None
    for c in range(LEFT_CHUNKS + DELAY):
        if c < LEFT_CHUNKS:
            rows = pl.ds(c * size, size)
            for copy in copies[c]:
                copy.wait()
            merged_ref[:, rows] = merged_ref[:, rows] + buffer[:, rows]
            outs.append(
                pltpu.make_async_copy(
                    merged_ref.at[:, rows], merged_hbm.at[:, rows], out_sems.at[c]
                )
            )
            outs[-1].start()
        if c == DELAY:
            small[0].wait()
            q = q_buffer[...]
            q_high = q.astype(bf16).astype(f32)
            right = jnp.concatenate([q_high, q - q_high], axis=0).T.astype(bf16)
        if c == LEFT_CHUNKS - 1:
            for n in range(3):
                small[n + 1].wait()
                states_ref[n] = state_buffer[n].astype(bf16)
            outs.append(pltpu.make_async_copy(states_ref, states_hbm, small_sems.at[4]))
            outs[-1].start()
        if c >= DELAY:
            rows = pl.ds((c - DELAY) * size, size)
            merged = merged_ref[:, rows].reshape(2 * size, COLS).astype(bf16)
            part = dot(merged, right, 1, 0)
            part = part + pltpu.roll(part, RANK, 1)
            part_ref[rows, :] = jnp.where(low_lanes, part[:size], part[size:]).astype(bf16)
    for copy in outs:
        copy.wait()


def left(grads, errors, q_init, master, m_state, v_state):
    return pl.pallas_call(
        left_kernel,
        out_shape=(
            pltpu.HBM((2, HALF, COLS), f32),
            jax.ShapeDtypeStruct((HALF, 2 * RANK), bf16),
            pltpu.HBM((3, ROWS, COLS), bf16),
        ),
        in_specs=[pl.BlockSpec(memory_space=pltpu.HBM)] * 6,
        out_specs=(
            pl.BlockSpec(memory_space=pltpu.HBM),
            pl.BlockSpec(memory_space=pltpu.VMEM),
            pl.BlockSpec(memory_space=pltpu.HBM),
        ),
        scratch_shapes=[
            pltpu.VMEM((2, HALF, COLS), f32),
            pltpu.VMEM((2, HALF, COLS), f32),
            pltpu.VMEM((RANK, COLS), f32),
            pltpu.VMEM((3, ROWS, COLS), f32),
            pltpu.VMEM((3, ROWS, COLS), bf16),
            pltpu.SemaphoreType.DMA((2, LEFT_CHUNKS)),
            pltpu.SemaphoreType.DMA((LEFT_CHUNKS,)),
            pltpu.SemaphoreType.DMA((5,)),
        ],
        compiler_params=pltpu.CompilerParams(vmem_limit_bytes=20 * MIB),
        name="left_factor",
    )(
        hbm(grads.reshape(2, HALF, COLS)), hbm(errors.reshape(2, HALF, COLS)), hbm(q_init.T),
        hbm(master), hbm(m_state), hbm(v_state),
    )


def sum_kernel(parts_ref, out_ref):
    total = jnp.sum(parts_ref[...].astype(f32).reshape(128, 8, 128), axis=0, keepdims=True)
    out_ref[...] = jnp.broadcast_to(total, out_ref.shape)


def sum_repeat(parts):
    return pl.pallas_call(
        sum_kernel,
        out_shape=jax.ShapeDtypeStruct((64, 8, 128), f32),
        in_specs=[pl.BlockSpec(memory_space=pltpu.VMEM)],
        out_specs=pl.BlockSpec(memory_space=pltpu.VMEM),
        compiler_params=pltpu.CompilerParams(vmem_limit_bytes=16 * MIB),
        name="sum_repeat",
    )(parts)


def inverse_factor(gram, after_panel):
    row_id = lax.broadcasted_iota(jnp.int32, (RANK, 2 * RANK), 0)
    lane = lanes((RANK, 2 * RANK))
    eye = jnp.where(row_id == lane, 1.0, 0.0).astype(f32)
    trace = jnp.sum(gram * eye, keepdims=True)
    jitter = 1e-06 * trace / RANK + 1e-06
    start = jnp.where(lane < RANK, gram + jitter * eye, jnp.where(row_id == lane - RANK, 1.0, 0.0))
    count = RANK // 8
    tiles = [start[8 * k : 8 * k + 8] for k in range(count)]
    sub = lax.broadcasted_iota(jnp.int32, (8, 2 * RANK), 0)
    for t in range(count):
        below = range(t, count)
        columns = {
            (c, k): jnp.broadcast_to(tiles[k][:, 8 * t + c : 8 * t + c + 1], sub.shape)
            for c in range(8)
            for k in below
        }
        for c in range(8):
            reciprocal = 1.0 / columns[c, t][c : c + 1]
            factors = {k: columns[c, k] * reciprocal for k in below}
            factors[t] = jnp.where(sub > c, factors[t], 0.0)
            for later in range(c + 1, 8):
                pivot_row = columns[later, t][c : c + 1]
                for k in below:
                    columns[later, k] = columns[later, k] - factors[k] * pivot_row
            pivot_row = tiles[t][c : c + 1]
            for k in below:
                tiles[k] = tiles[k] - factors[k] * pivot_row
        after_panel(t)
    done = jnp.concatenate(tiles, axis=0)
    pivots = jnp.sum(done * eye, axis=1, keepdims=True)
    return jnp.where(lane < RANK, 0.0, done * (1.0 / jnp.sqrt(pivots)))


def pair_rows(packed):
    low_lanes = lanes(packed.shape) < RANK
    high = packed.astype(bf16).astype(f32)
    low = packed - high
    top = jnp.where(low_lanes, high, pltpu.roll(low, RANK, 1)).astype(bf16)
    bottom = jnp.where(low_lanes, pltpu.roll(high, RANK, 1), low).astype(bf16)
    return top, bottom


def pair_gram(halves):
    square = sum(dot(half, half, 0, 0) for half in halves)
    square = square[:RANK] + square[RANK:]
    return square + pltpu.roll(square, RANK, 1)


def right_kernel(own_ref, other_ref, merged_hbm, orth_ref, square_ref, part_ref, merged_ref, sems):
    def copy(c):
        half, rows = c // 4, pl.ds(c % 4 * BLOCK, BLOCK)
        return pltpu.make_async_copy(
            merged_hbm.at[half, rows], merged_ref.at[half, rows], sems.at[c]
        )

    for c in range(RIGHT_AHEAD):
        copy(c).start()
    own, other = own_ref[...], other_ref[...]
    first = lax.axis_index("c") == 0
    packed = jnp.concatenate([jnp.where(first, own, other), jnp.where(first, other, own)], axis=0)
    pairs = pair_rows(packed)
    acc = [jnp.zeros((2 * RANK, COLS), f32)]

    def multiply(c):
        copy(c).wait()
        if c + RIGHT_AHEAD < D // BLOCK:
            copy(c + RIGHT_AHEAD).start()
        half, rows = c // 4, pl.ds(c % 4 * BLOCK, BLOCK)
        left = pairs[half][c % 4 * BLOCK : (c % 4 + 1) * BLOCK]
        acc[0] = acc[0] + dot(left, merged_ref[half, rows].astype(bf16), 0, 0)

    inverse = inverse_factor(pair_gram(pairs), multiply)
    part = acc[0][:RANK] + acc[0][RANK:]

    flipped = pltpu.roll(inverse, RANK, 1)
    inverse_small = flipped[:, :RANK]
    part_ref[...] = (dot(inverse_small, part, 1, 0, HIGHEST) * (1.0 / REPLICAS)).astype(bf16)

    high = inverse_small.astype(bf16).astype(f32)
    factor = jnp.concatenate([high, inverse_small - high], axis=0).T
    factor = jnp.concatenate([factor, factor], axis=0).astype(bf16)
    halves = []
    low_lanes = lanes((HALF, 2 * RANK)) < RANK
    for half in range(2):
        orth = dot(pairs[half], factor, 1, 0)
        orth = orth + pltpu.roll(orth, RANK, 1)
        high = orth.astype(bf16).astype(f32)
        pair = jnp.where(low_lanes, high, orth - high).astype(bf16)
        orth_ref[half * HALF : (half + 1) * HALF] = pair
        halves.append(pair)
    square_ref[...] = pair_gram(halves)


def right(own, other, merged):
    return pl.pallas_call(
        right_kernel,
        out_shape=(
            jax.ShapeDtypeStruct((D, 2 * RANK), bf16),
            jax.ShapeDtypeStruct((RANK, 2 * RANK), f32),
            jax.ShapeDtypeStruct((RANK, COLS), bf16),
        ),
        in_specs=[
            pl.BlockSpec(memory_space=pltpu.VMEM),
            pl.BlockSpec(memory_space=pltpu.VMEM),
            pl.BlockSpec(memory_space=pltpu.HBM),
        ],
        out_specs=(pl.BlockSpec(memory_space=pltpu.VMEM),) * 3,
        scratch_shapes=[
            pltpu.VMEM((2, HALF, COLS), f32),
            pltpu.SemaphoreType.DMA((D // BLOCK,)),
        ],
        compiler_params=pltpu.CompilerParams(vmem_limit_bytes=16 * MIB),
        name="right_factor",
    )(own, other, hbm(merged))


def adam(update, master, m_state, v_state):
    m_new = beta_first * m_state + (1.0 - beta_first) * update
    v_new = beta_second * v_state + (1.0 - beta_second) * update * update
    m_hat = m_new / (1.0 - beta_first**STEP)
    v_hat = v_new / (1.0 - beta_second**STEP)
    master_new = master * (1.0 - learning_rate * decay_weight) - learning_rate * m_hat / (
        jnp.sqrt(v_hat) + adam_eps
    )
    return m_new, v_new, master_new


def new_weights(update, master, m_state, v_state):
    first = learning_rate / (1.0 - beta_first**STEP)
    second = 1.0 / (1.0 - beta_second**STEP)
    top = (first * beta_first) * m_state + (first * (1.0 - beta_first)) * update
    square = (second * beta_second) * v_state + (second * (1.0 - beta_second)) * (update * update)
    root = square * lax.rsqrt(square) + adam_eps
    return (1.0 - learning_rate * decay_weight) * master - top * pl.reciprocal(root, approx=True)


def final_kernel(
    q_ref, orth_ref, square_ref, merged_hbm, states_hbm, master_ref, m_ref, v_ref,
    error_hbm, weights_hbm, q_hbm, master_hbm, m_hbm, v_hbm,
    states_ref, merged_ref, error_ref, weights_ref, q_out, owned_ref, both_ref,
    in_sems, merged_sems, error_sems, weight_sems, small_sems,
):
    steps = D // BLOCK
    per = BLOCK // ROWS

    def states_copy(c):
        part = pl.ds(c * per, per)
        return pltpu.make_async_copy(states_hbm.at[part], states_ref.at[part], in_sems.at[c])

    def merged_copy(c):
        half = c // (steps // 2)
        rows = pl.ds(pl.multiple_of((c - half * (steps // 2)) * BLOCK, BLOCK), BLOCK)
        whole = pl.ds(pl.multiple_of(c * BLOCK, BLOCK), BLOCK)
        return pltpu.make_async_copy(
            merged_hbm.at[half, rows], merged_ref.at[whole], merged_sems.at[c]
        )

    def out_copies(c):
        rows = pl.ds(pl.multiple_of(c * BLOCK, BLOCK), BLOCK)
        return (
            pltpu.make_async_copy(error_ref.at[rows], error_hbm.at[rows], error_sems.at[c]),
            pltpu.make_async_copy(weights_ref.at[rows], weights_hbm.at[rows], weight_sems.at[c]),
        )

    for c in range(AHEAD):
        merged_copy(c).start()
        states_copy(c).start()
    gram = jnp.zeros((RANK, RANK), f32)
    for z in range(4):
        gram = gram + dot(q_ref[z], q_ref[z], 1, 1)
    total = jnp.sum(gram * square_ref[:, :RANK], keepdims=True)
    scale = 1.0 / jnp.sqrt(total / (D * HID) + norm_eps)
    q = q_ref[lax.axis_index("z")]
    both_ref[:RANK] = q
    both_ref[RANK:] = q
    q_out[...] = q.astype(f32)
    start = pl.multiple_of(lax.axis_index(DP) * ROWS, ROWS)
    decoded = dot(orth_ref[pl.ds(start, ROWS)], both_ref[...], 1, 0)
    owned = adam(decoded * scale, master_ref[...], m_ref[...], v_ref[...])
    small = [pltpu.make_async_copy(q_out, q_hbm, small_sems.at[3])]
    for n, target in enumerate((m_hbm, v_hbm, master_hbm)):
        owned_ref[n] = owned[n]
        small.append(pltpu.make_async_copy(owned_ref.at[n], target, small_sems.at[n]))
    for copy in small:
        copy.start()

    @pl.loop(0, steps)
    def _(c):
        rows = pl.ds(pl.multiple_of(c * BLOCK, BLOCK), BLOCK)
        decoded = dot(orth_ref[rows], both_ref[...], 1, 0)
        merged_copy(c).wait()

        @pl.when(c + AHEAD < steps)
        def _():
            merged_copy(c + AHEAD).start()
            states_copy(c + AHEAD).start()

        error_ref[rows] = merged_ref[rows] - decoded
        update = decoded * scale
        states_copy(c).wait()
        for k in range(per):
            state = [states_ref[c * per + k, n].astype(f32) for n in range(3)]
            block = pl.ds(pl.multiple_of(c * BLOCK + k * ROWS, ROWS), ROWS)
            weights_ref[block] = new_weights(update[k * ROWS : (k + 1) * ROWS], *state).astype(bf16)
        for copy in out_copies(c):
            copy.start()

    for c in range(steps):
        for copy in out_copies(c):
            copy.wait()
    for copy in small:
        copy.wait()


def final(q_all, orth, square, merged, states, master, m_state, v_state):
    steps = D // BLOCK
    return pl.pallas_call(
        final_kernel,
        out_shape=(
            jax.ShapeDtypeStruct((D, COLS), f32),
            jax.ShapeDtypeStruct((D, COLS), bf16),
            jax.ShapeDtypeStruct((RANK, COLS), f32),
            jax.ShapeDtypeStruct((ROWS, COLS), f32),
            jax.ShapeDtypeStruct((ROWS, COLS), f32),
            jax.ShapeDtypeStruct((ROWS, COLS), f32),
        ),
        in_specs=[pl.BlockSpec(memory_space=pltpu.VMEM)] * 3
        + [pl.BlockSpec(memory_space=pltpu.HBM)] * 2
        + [pl.BlockSpec(memory_space=pltpu.VMEM)] * 3,
        out_specs=(pl.BlockSpec(memory_space=pl.ANY),) * 6,
        scratch_shapes=[
            pltpu.VMEM((REPLICAS, 3, ROWS, COLS), bf16),
            pltpu.VMEM((D, COLS), f32),
            pltpu.VMEM((D, COLS), f32),
            pltpu.VMEM((D, COLS), bf16),
            pltpu.VMEM((RANK, COLS), f32),
            pltpu.VMEM((3, ROWS, COLS), f32),
            pltpu.VMEM((2 * RANK, COLS), bf16),
            pltpu.SemaphoreType.DMA((steps,)),
            pltpu.SemaphoreType.DMA((steps,)),
            pltpu.SemaphoreType.DMA((steps,)),
            pltpu.SemaphoreType.DMA((steps,)),
            pltpu.SemaphoreType.DMA((4,)),
        ],
        compiler_params=pltpu.CompilerParams(vmem_limit_bytes=32 * MIB),
        name="decode_update",
    )(q_all, orth, square, hbm(merged), hbm(states), master, m_state, v_state)


def shards(grads, errors, q_init, master, m_state, v_state):
    merged, part, states = left(grads, errors, q_init, master, m_state, v_state)
    states = lax.all_gather(states, DP, axis=0, tiled=False)
    parts = lax.all_to_all(part.reshape(128, 8, 128), ("c", "y", "x", "z"), 0, 0)
    owned = sum_repeat(parts.reshape(HALF, 128))
    own = lax.all_to_all(owned, ("y", "x", "z"), 0, 0).reshape(HALF // 2, 128)
    other = lax.ppermute(own, "c", [(0, 1), (1, 0)])
    orth, square, q_part = right(own, other, merged)
    q_parts = lax.all_to_all(q_part.reshape(32, 2, COLS), DP, 0, 0)
    q_owned = jnp.sum(q_parts.astype(f32), axis=0).astype(bf16)
    q_owned = jnp.broadcast_to(q_owned[None], (128, 2, COLS))
    q_all = lax.all_to_all(q_owned, ("z",) + DP, 0, 0).reshape(4, RANK, COLS)
    error_new, weights, q_new, master_new, m_new, v_new = final(
        q_all, orth, square, merged, states, master, m_state, v_state
    )
    return (error_new[None], q_new.T, master_new, m_new, v_new, weights)


def solution(mesh):
    replicas, columns = mesh.devices.shape
    mesh = Mesh(mesh.devices.reshape(4, replicas // 8, 2, columns), DP + ("z",))
    in_specs = (
        P(DP, None, "z"),
        P(DP, None, "z"),
        P("z", None),
        P(DP, "z"),
        P(DP, "z"),
        P(DP, "z"),
    )
    out_specs = (
        P(DP, None, "z"),
        P("z", None),
        P(DP, "z"),
        P(DP, "z"),
        P(DP, "z"),
        P(None, "z"),
    )
    return jax.shard_map(shards, mesh=mesh, in_specs=in_specs, out_specs=out_specs, check_vma=False)
```
